128 devices in a mesh: rows: 16 (over y, x_hi, core), cols: 8 (over x_lo, z).
Axes of the slice: x: 4 (x_hi: 2, x_lo: 2; x = x_hi * 2 + x_lo), y: 4, z: 4, core: 2. Of those that a mesh axis runs over, the one named last changes fastest.
Arguments:
- frame: float32 [1024, 8192], P(('rows', 'cols')), may hold values from -6 to 6
- taps_row: float32 [15], replicated, may hold values from -1.5 to 1.5
- taps_col: float32 [15], replicated, may hold values from -1.5 to 1.5
- merit: bfloat16 [64, 1024, 8192], P(None, 'rows', 'cols'), may hold values from -9 to 9
- offsets: int32 [64, 2], replicated, may hold values from -8 to 8, as said below
Outputs:
- merit_next: bfloat16 [64, 1024, 8192], P(None, 'rows', 'cols')
The draws below stay inside these ranges and needn't reach their ends.
Inputs may be any that keep to these rules, and one draw needn't show every extreme that they name: `offsets`: each component of every shift lies in -8 .. 8; some velocity has shift (-8, 8) and some other one (8, -8).
All inputs are finite; a program needn't handle non-finite values.
Results may differ from the reference program's by a relative error of at most 0.001.
Values may be sent and summed in bfloat16 or wider, within the bound.
No kernel may reach another device: no remote copies, remote signals or barrier semaphores. Data moves between devices by JAX's collectives and lax.ppermute only.
A program may use at most 192 MiB of HBM per device.

```python
import jax
import jax.numpy as jnp
from jax import lax

W = 8192
TAPS = 15
VGRID = 8
MAXV = 8
VELS = 64
H = 1024


def draw_offsets(key, part):
    base = jax.random.randint(key, (VGRID * VGRID, 2), -MAXV, MAXV + 1).astype(jnp.int32)
    where = jax.random.randint(jax.random.fold_in(key, 7), (), 0, VGRID * VGRID - 1).astype(jnp.int32)
    first = jnp.array([-MAXV, MAXV], jnp.int32)
    second = jnp.array([MAXV, -MAXV], jnp.int32)
    base = base.at[where].set(first)
    base = base.at[where + 1].set(second)
    return base.astype(jnp.int32)


def shard_levels(rng, extent, pieces, least, largest):
    level = 1.0
    for dim, shards_of in pieces:
        draws = jax.random.uniform(jax.random.fold_in(jax.random.fold_in(rng, 6), dim), (shards_of,), jnp.float32, least / len(pieces), largest / len(pieces))
        level = level * jnp.repeat(jnp.exp(draws), extent[dim] // shards_of).reshape((-1,) + (1,) * (len(extent) - 1 - dim))
    return level


def bell_draw(rng, extent, width, bound, pieces=(), kind=jnp.bfloat16):
    values = jax.random.normal(rng, extent, jnp.float32) * width
    if len(pieces) > 0:
        values = shard_levels(rng, extent, pieces, -0.22, 0.18) * values
    return jnp.clip(values, min=-bound, max=bound).astype(kind)


def setup_inputs(seed: int = 0) -> dict:
    splits = jax.random.split(jax.random.key(seed), 6)
    frame = bell_draw(splits[0], (H, W), 1.0, 6.0, ((0, 128),), jnp.float32)
    taps_row = bell_draw(splits[1], (TAPS,), 15 ** -0.5, 1.5, (), jnp.float32)
    taps_col = bell_draw(splits[2], (TAPS,), 15 ** -0.5, 1.5, (), jnp.float32)
    merit = bell_draw(splits[3], (VELS, H, W), 1.5, 9.0, ((1, 16), (2, 8)))
    offsets = draw_offsets(jax.random.fold_in(splits[5], 71), 0)
    return {"frame": frame, "taps_row": taps_row, "taps_col": taps_col, "merit": merit, "offsets": offsets}


def reference(frame, taps_row, taps_col, merit, offsets):
    half = TAPS // 2
    padded = jnp.pad(frame, ((0, 0), (half, half)))
    horiz = jnp.zeros(frame.shape, jnp.float32)
    for j in range(TAPS):
        horiz = horiz + taps_row[j] * padded[:, j:j + W]
    padded = jnp.pad(horiz, ((half, half), (0, 0)))
    filtered = jnp.zeros(frame.shape, jnp.float32)
    for i in range(TAPS):
        filtered = filtered + taps_col[i] * padded[i:i + H, :]

    def one_plane(index):
        row_pos = index // VGRID
        col_pos = index % VGRID
        best = merit[index]
        for drow in (-1, 0, 1):
            for dcol in (-1, 0, 1):
                other_row = jnp.clip(row_pos + drow, 0, VGRID - 1)
                other_col = jnp.clip(col_pos + dcol, 0, VGRID - 1)
                best = jnp.maximum(best, merit[other_row * VGRID + other_col])
        wide = jnp.pad(best, ((MAXV, MAXV), (MAXV, MAXV)))
        start_row = (MAXV - offsets[index, 0]).astype(jnp.int32)
        start_col = (MAXV - offsets[index, 1]).astype(jnp.int32)
        moved = lax.dynamic_slice(wide, (start_row, start_col), (H, W))
        return (filtered + 0.875 * moved.astype(jnp.float32)).astype(jnp.bfloat16)

    return lax.map(one_plane, jnp.arange(VELS, dtype=jnp.int32))
```

```python
import functools

import jax
import jax.numpy as jnp
from jax import lax
from jax.experimental import pallas as pl
from jax.experimental.pallas import tpu as pltpu
from jax.sharding import PartitionSpec as P

VGRID = 8
MAXV = 8
VELS = VGRID * VGRID
LANES = 128
FORGET = 0.875
SEAM = 16
SOME_ROWS = 192
ALL_ROWS = VELS * MAXV
LIMIT = 56 * 2**20

f32 = jnp.float32
bf16 = jnp.bfloat16


def params(limit=LIMIT):
    return pltpu.CompilerParams(vmem_limit_bytes=limit)


def smem():
    return pl.BlockSpec(memory_space=pltpu.SMEM)


def filter_rows_kernel(taps_ref, strip_ref, out_ref, pad_ref):
    half = taps_ref.shape[0] // 2
    height, width = strip_ref.shape
    pad_ref[:, :LANES] = jnp.zeros((height, LANES), f32)
    pad_ref[:, LANES + width :] = jnp.zeros((height, LANES), f32)
    pad_ref[:, LANES : LANES + width] = strip_ref[...]
    count, _, span = out_ref.shape
    for piece in range(count):
        start = LANES + piece * span
        total = jnp.zeros((height, span), f32)
        for j in range(taps_ref.shape[0]):
            total = total + taps_ref[j] * pad_ref[:, start + j - half : start + j - half + span]
        out_ref[piece] = total


def filter_rows(strip, taps_row, pieces):
    height, width = strip.shape
    return pl.pallas_call(
        filter_rows_kernel,
        out_shape=jax.ShapeDtypeStruct((pieces, height, width // pieces), f32),
        in_specs=[smem(), pl.BlockSpec(memory_space=pltpu.VMEM)],
        out_specs=pl.BlockSpec(memory_space=pltpu.VMEM),
        scratch_shapes=[pltpu.VMEM((height, width + 2 * LANES), f32)],
        compiler_params=params(),
        name="filter_rows",
    )(taps_row, strip)


def max_of_three(values):
    total = len(values)
    pairs = [jnp.maximum(values[i], values[i + 1]) for i in range(total - 1)]
    middle = [jnp.maximum(pairs[i - 1], values[i + 1]) for i in range(1, total - 1)]
    return [pairs[0]] + middle + [pairs[-1]]


def pool_kernel(rows, offsets_ref, merit_ref, pooled_ref, right_ref, left_ref, down_ref, up_ref, bottom_ref, top_ref):
    step = pl.program_id(0)
    steps = pl.num_programs(0)
    _, height, width = merit_ref.shape
    blocks = width // LANES

    def pool_block(k, carry):
        cols = pl.ds(pl.multiple_of(k * LANES, LANES), LANES)

        def line(a):
            return max_of_three([merit_ref[a * VGRID + b, :, cols] for b in range(VGRID)])

        def emit(a, planes):
            for b in range(VGRID):
                pooled_ref[a * VGRID + b, :, cols] = planes[b]

        last, here = line(0), line(1)
        pair = [jnp.maximum(x, y) for x, y in zip(last, here)]
        emit(0, pair)
        for a in range(2, VGRID):
            after = line(a)
            emit(a - 1, [jnp.maximum(x, y) for x, y in zip(pair, after)])
            pair = [jnp.maximum(x, y) for x, y in zip(here, after)]
            here = after
        emit(VGRID - 1, pair)
        return carry

    lax.fori_loop(0, blocks, pool_block, 0)

    lane_group = lax.broadcasted_iota(jnp.int32, (height, LANES), 1) // MAXV
    share = LANES // MAXV
    for g in range(VELS // share):
        right = jnp.zeros((height, LANES), f32)
        left = jnp.zeros((height, LANES), f32)
        for w in range(share):
            v = g * share + w
            last = pooled_ref[v, :, width - LANES :].astype(f32)
            first = pooled_ref[v, :, :LANES].astype(f32)
            right = jnp.where(lane_group == w, pltpu.roll(last, (w + 1) * MAXV % LANES, 1), right)
            left = jnp.where(lane_group == w, pltpu.roll(first, w * MAXV, 1), left)
        right_ref[g] = right.astype(bf16)
        left_ref[g] = left.astype(bf16)

    @pl.when(step == 0)
    def _():
        def pack(v, at):
            for k in range(blocks):
                tile = pooled_ref[v, :, k * LANES : (k + 1) * LANES].astype(f32)
                top_ref[k, pl.ds(at + MAXV, MAXV), :] = tile[:MAXV]
            return at + jnp.maximum(-offsets_ref[v, 0], 0)

        lax.fori_loop(0, VELS, pack, 0)
        for k in range(blocks):
            up_ref[SEAM:, k * LANES : (k + 1) * LANES] = top_ref[k, MAXV : MAXV + rows, :].astype(bf16)

    @pl.when(step == steps - 1)
    def _():
        def count(v, total):
            return total + jnp.maximum(offsets_ref[v, 0], 0)

        def pack(i, at):
            v = VELS - 1 - i
            for k in range(blocks):
                tile = pooled_ref[v, :, k * LANES : (k + 1) * LANES].astype(f32)
                bottom_ref[k, pl.ds(at, MAXV), :] = tile[height - MAXV :]
            return at - jnp.maximum(offsets_ref[v, 0], 0)

        lax.fori_loop(0, VELS, pack, lax.fori_loop(0, VELS, count, 0))
        for k in range(blocks):
            down_ref[SEAM:, k * LANES : (k + 1) * LANES] = bottom_ref[k, MAXV : MAXV + rows, :].astype(bf16)


def pool(merit, offsets, rows):
    planes, height, width = merit.shape
    chunk = 16
    blocks = width // LANES
    groups = planes * MAXV // LANES
    whole = pl.BlockSpec((SEAM + rows, width), lambda i: (0, 0))
    sides = pl.BlockSpec((groups, chunk, LANES), lambda i: (0, i, 0))
    return pl.pallas_call(
        functools.partial(pool_kernel, rows),
        grid=(height // chunk,),
        out_shape=[
            jax.ShapeDtypeStruct(merit.shape, bf16),
            jax.ShapeDtypeStruct((groups, height, LANES), bf16),
            jax.ShapeDtypeStruct((groups, height, LANES), bf16),
            jax.ShapeDtypeStruct((SEAM + rows, width), bf16),
            jax.ShapeDtypeStruct((SEAM + rows, width), bf16),
        ],
        in_specs=[smem(), pl.BlockSpec((planes, chunk, width), lambda i: (0, i, 0))],
        out_specs=[pl.BlockSpec((planes, chunk, width), lambda i: (0, i, 0)), sides, sides, whole, whole],
        scratch_shapes=[pltpu.VMEM((blocks, ALL_ROWS + 2 * MAXV, LANES), f32)] * 2,
        cost_estimate=pl.CostEstimate(flops=4 * merit.size, bytes_accessed=4 * merit.size, transcendentals=0),
        compiler_params=params(),
        name="pool",
    )(offsets, merit)


def seam_kernel(tile_ref, down_in, up_in, down_ref, up_ref, buf_ref, sems):
    del down_in, up_in
    height = tile_ref.shape[0]
    for i, (edge, target) in enumerate(((tile_ref[height - MAXV :, :], down_ref), (tile_ref[:MAXV, :], up_ref))):
        lead = edge.astype(bf16).astype(f32)
        buf_ref[i] = jnp.concatenate([lead, edge - lead], axis=0).astype(bf16)
    copies = [
        pltpu.make_async_copy(buf_ref.at[i], target.at[pl.ds(0, SEAM), :], sems.at[i])
        for i, target in enumerate((down_ref, up_ref))
    ]
    for copy in copies:
        copy.start()
    for copy in copies:
        copy.wait()


def add_seam(tile, down, up):
    anywhere = pl.BlockSpec(memory_space=pl.ANY)
    return pl.pallas_call(
        seam_kernel,
        out_shape=[jax.ShapeDtypeStruct(down.shape, bf16), jax.ShapeDtypeStruct(up.shape, bf16)],
        in_specs=[pl.BlockSpec(memory_space=pltpu.VMEM), anywhere, anywhere],
        out_specs=[anywhere, anywhere],
        input_output_aliases={1: 0, 2: 1},
        scratch_shapes=[pltpu.VMEM((2, SEAM, tile.shape[1]), bf16), pltpu.SemaphoreType.DMA((2,))],
        compiler_params=params(),
        name="add_seam",
    )(tile, down, up)


def merge_kernel(
    rows, offsets_ref, taps_ref, pooled_ref, tile_ref, above_ref, below_ref, west_ref, east_ref, out_ref,
    halo_ref, side_ref, column_ref, filtered_ref, moved_ref, at_ref,
):
    step = pl.program_id(0)
    planes, height, width = pooled_ref.shape
    blocks = width // LANES
    groups = VELS * MAXV // LANES
    share = LANES // MAXV

    @pl.when(step == 0)
    def _():
        at_ref[0] = 0
        at_ref[1] = 0
        near = groups * height
        for e, ref in enumerate((above_ref, below_ref)):
            for k in range(blocks):
                halo_ref[e, k + 1, MAXV : MAXV + rows, :] = ref[SEAM:, k * LANES : (k + 1) * LANES].astype(f32)
            start = near + e * rows
            halo_ref[e, 0, MAXV : MAXV + rows, :] = west_ref[start : start + rows, :].astype(f32)
            halo_ref[e, blocks + 1, MAXV : MAXV + rows, :] = east_ref[start : start + rows, :].astype(f32)
        for e, ref in enumerate((west_ref, east_ref)):
            for g in range(groups):
                side_ref[e, g] = ref[g * height : (g + 1) * height, :].astype(f32)
        half = taps_ref.shape[0] // 2
        for k in range(blocks):
            cols = slice(k * LANES, (k + 1) * LANES)
            over = above_ref[:SEAM, cols].astype(f32)
            under = below_ref[:SEAM, cols].astype(f32)
            column_ref[k, :MAXV, :] = over[:MAXV] + over[MAXV:]
            column_ref[k, MAXV : MAXV + height, :] = tile_ref[:, cols]
            column_ref[k, MAXV + height :, :] = under[:MAXV] + under[MAXV:]
        for k in range(blocks):
            total = jnp.zeros((height, LANES), f32)
            for i in range(taps_ref.shape[0]):
                start = MAXV - half + i
                total = total + taps_ref[i] * column_ref[k, start : start + height, :]
            filtered_ref[k] = total

    moves = []
    for p in range(planes):
        v = step * planes + p
        dy = offsets_ref[v, 0]
        dx = offsets_ref[v, 1]
        turn = dx & (LANES - 1)
        west = dx >= 0
        q = jnp.where(west, 0, 1)
        moves.append((dy, turn, q))
        for k in range(blocks):
            here = pooled_ref[p, :, k * LANES : (k + 1) * LANES].astype(f32)
            moved_ref[p, k + 1, MAXV : MAXV + height, :] = pltpu.roll(here, turn, 1)
        g, w = v // share, v % share
        shift = (turn - w * MAXV - jnp.where(west, MAXV, 0) + 2 * LANES) & (LANES - 1)
        moved_ref[p, q * (blocks + 1), MAXV : MAXV + height, :] = pltpu.roll(side_ref[q, g], shift, 1)
        e = jnp.where(dy >= 0, 0, 1)
        source = jnp.where(dy >= 0, at_ref[0] + dy, at_ref[1] + MAXV)
        target = pl.multiple_of(e * (MAXV + height), MAXV)
        for k in range(blocks + 2):
            edge = halo_ref[e, k, pl.ds(source, MAXV), :]
            moved_ref[p, k, pl.ds(target, MAXV), :] = pltpu.roll(edge, turn, 1)
        at_ref[0] += jnp.maximum(dy, 0)
        at_ref[1] += jnp.maximum(-dy, 0)

    lane = lax.broadcasted_iota(jnp.int32, (height, LANES), 1)
    for p in range(planes):
        dy, turn, q = moves[p]
        window = pl.ds(MAXV - dy, height)
        for k in range(blocks):
            one = moved_ref[p, k + q, window, :]
            two = moved_ref[p, k + 1 + q, window, :]
            total = filtered_ref[k] + FORGET * jnp.where(lane < turn, one, two)
            out_ref[p, :, k * LANES : (k + 1) * LANES] = total.astype(bf16)


def merge(pooled, tile, above, below, west, east, offsets, taps_col):
    planes, height, width = pooled.shape
    rows = above.shape[0] - SEAM
    blocks = width // LANES
    groups = planes * MAXV // LANES
    slab = pl.BlockSpec((VGRID, height, width), lambda i: (i, 0, 0))

    def whole(array):
        return pl.BlockSpec(array.shape, lambda i: (0, 0))

    return pl.pallas_call(
        functools.partial(merge_kernel, rows),
        grid=(planes // VGRID,),
        out_shape=jax.ShapeDtypeStruct(pooled.shape, bf16),
        in_specs=[smem(), smem(), slab] + [whole(a) for a in (tile, above, below, west, east)],
        out_specs=slab,
        scratch_shapes=[
            pltpu.VMEM((2, blocks + 2, rows + 2 * MAXV, LANES), f32),
            pltpu.VMEM((2, groups, height, LANES), f32),
            pltpu.VMEM((blocks, height + 2 * MAXV, LANES), f32),
            pltpu.VMEM((blocks, height, LANES), f32),
            pltpu.VMEM((VGRID, blocks + 2, height + 2 * MAXV, LANES), f32),
            pltpu.SMEM((2,), jnp.int32),
        ],
        compiler_params=params(),
        name="merge",
    )(offsets, taps_col, pooled, tile, above, below, west, east)


def pass_on(value, axis):
    count = lax.axis_size(axis)
    return lax.ppermute(value, axis, [(i, i + 1) for i in range(count - 1)])


def pass_back(value, axis):
    count = lax.axis_size(axis)
    return lax.ppermute(value, axis, [(i + 1, i) for i in range(count - 1)])


def step_with(rows, frame, taps_row, taps_col, merit, offsets):
    _, height, width = merit.shape
    pieces = filter_rows(frame, taps_row, frame.shape[1] // width)
    tile = lax.all_to_all(pieces, "cols", split_axis=0, concat_axis=0, tiled=True).reshape(height, width)
    pooled, right, left, down, up = pool(merit, offsets, rows)
    down, up = add_seam(tile, down, up)
    above = pass_on(down, "rows")
    below = pass_back(up, "rows")
    last = [right.reshape(-1, LANES), above[SEAM:, width - LANES :], below[SEAM:, width - LANES :]]
    first = [left.reshape(-1, LANES), above[SEAM:, :LANES], below[SEAM:, :LANES]]
    west = pass_on(jnp.concatenate(last, axis=0), "cols")
    east = pass_back(jnp.concatenate(first, axis=0), "cols")
    return merge(pooled, tile, above, below, west, east, offsets, taps_col)


def on_device(frame, taps_row, taps_col, merit, offsets):
    shifts = offsets[:, 0]
    most = jnp.maximum(jnp.sum(jnp.maximum(shifts, 0)), jnp.sum(jnp.maximum(-shifts, 0)))
    return lax.cond(
        most <= SOME_ROWS,
        functools.partial(step_with, SOME_ROWS),
        functools.partial(step_with, ALL_ROWS),
        frame, taps_row, taps_col, merit, offsets,
    )


def solution(mesh):
    in_specs = (P(("rows", "cols"), None), P(), P(), P(None, "rows", "cols"), P())
    out_specs = P(None, "rows", "cols")
    return jax.shard_map(on_device, mesh=mesh, in_specs=in_specs, out_specs=out_specs, check_vma=False)
```

```python
import functools

import jax
import jax.numpy as jnp
from jax import lax
from jax.experimental import pallas as pl
from jax.experimental.pallas import tpu as pltpu
from jax.sharding import PartitionSpec as P

VGRID = 8
MAXV = 8
VELS = VGRID * VGRID
LANES = 128
FORGET = 0.875
SOME_ROWS = 192
ALL_ROWS = VELS * MAXV
SLAB = 8
CHUNK = 16
LIMIT = 58 * 2**20

f32 = jnp.float32
bf16 = jnp.bfloat16


def params(limit=LIMIT):
    return pltpu.CompilerParams(vmem_limit_bytes=limit)


def smem():
    return pl.BlockSpec(memory_space=pltpu.SMEM)


def filter_rows_kernel(taps_ref, strip_ref, after_ref, out_ref, pad_ref):
    del after_ref
    half = taps_ref.shape[0] // 2
    height, width = strip_ref.shape
    pad_ref[:, :LANES] = jnp.zeros((height, LANES), f32)
    pad_ref[:, LANES + width :] = jnp.zeros((height, LANES), f32)
    pad_ref[:, LANES : LANES + width] = strip_ref[...]
    count, _, span = out_ref.shape
    for piece in range(count):
        start = LANES + piece * span
        total = jnp.zeros((height, span), f32)
        for j in range(taps_ref.shape[0]):
            total = total + taps_ref[j] * pad_ref[:, start + j - half : start + j - half + span]
        out_ref[piece] = total


def filter_rows(strip, taps_row, pieces, after):
    height, width = strip.shape
    return pl.pallas_call(
        filter_rows_kernel,
        out_shape=jax.ShapeDtypeStruct((pieces, height, width // pieces), f32),
        in_specs=[smem(), pl.BlockSpec(memory_space=pltpu.VMEM), pl.BlockSpec(memory_space=pl.ANY)],
        out_specs=pl.BlockSpec(memory_space=pltpu.VMEM),
        scratch_shapes=[pltpu.VMEM((height, width + 2 * LANES), f32)],
        compiler_params=params(),
        name="filter_rows",
    )(taps_row, strip, after)


def max_of_three(values):
    total = len(values)
    pairs = [jnp.maximum(values[i], values[i + 1]) for i in range(total - 1)]
    middle = [jnp.maximum(pairs[i - 1], values[i + 1]) for i in range(1, total - 1)]
    return [pairs[0]] + middle + [pairs[-1]]


def pool_chunk(merit_ref, pooled_ref, rows, cols):
    def line(a):
        return max_of_three([merit_ref[a * VGRID + b, rows, cols] for b in range(VGRID)])

    def emit(a, planes):
        for b in range(VGRID):
            pooled_ref[a * VGRID + b, rows, cols] = planes[b]

    last, here = line(0), line(1)
    pair = [jnp.maximum(x, y) for x, y in zip(last, here)]
    emit(0, pair)
    for a in range(2, VGRID):
        after = line(a)
        emit(a - 1, [jnp.maximum(x, y) for x, y in zip(pair, after)])
        pair = [jnp.maximum(x, y) for x, y in zip(here, after)]
        here = after
    emit(VGRID - 1, pair)


def pack_side(pooled_ref, cols, turn, target_ref):
    height = pooled_ref.shape[1]
    lane_group = lax.broadcasted_iota(jnp.int32, (height, LANES), 1) // MAXV
    share = LANES // MAXV
    for g in range(VELS // share):
        total = jnp.zeros((height, LANES), f32)
        for w in range(share):
            edge = pooled_ref[g * share + w, :, cols].astype(f32)
            total = jnp.where(lane_group == w, pltpu.roll(edge, (w + turn) * MAXV % LANES, 1), total)
        target_ref[g] = total.astype(bf16)


def pool_as_they_come(copies, sizes, held_ref, pooled_ref, then=None):
    for copy in copies:
        copy.start()
    for copy, (height, top, width, left) in zip(copies, sizes):
        copy.wait()
        across = width // LANES

        def one(i, carry):
            rows = pl.ds(pl.multiple_of(top + i // across * CHUNK, CHUNK), CHUNK)
            cols = pl.ds(pl.multiple_of(left + i % across * LANES, LANES), LANES)
            pool_chunk(held_ref, pooled_ref, rows, cols)
            return carry

        lax.fori_loop(0, height // CHUNK * across, one, 0)
        if then is not None:
            then(top, left)


def pool_all_kernel(merit_ref, *refs):
    pooled_ref, held_ref, sems = refs[-3:]
    _, height, width = merit_ref.shape
    part = width // 2
    sizes = [(CHUNK, top, part, left) for top in range(0, height, CHUNK) for left in (0, part)]
    copies = []
    for n, (_, top, _, left) in enumerate(sizes):
        at = (slice(None), pl.ds(top, CHUNK), pl.ds(left, part))
        copies.append(pltpu.make_async_copy(merit_ref.at[at], held_ref.at[at], sems.at[n]))
    pool_as_they_come(copies, sizes, held_ref, pooled_ref)


def pool_sides_kernel(merit_ref, after_ref, right_ref, left_ref, held_ref, pooled_ref, sems):
    del after_ref
    _, height, width = merit_ref.shape
    sizes = [(height, 0, LANES, left) for left in (0, LANES)]
    copies = []
    for n, first in enumerate((0, width - LANES)):
        source = merit_ref.at[:, :, pl.ds(first, LANES)]
        copies.append(pltpu.make_async_copy(source, held_ref.at[:, :, pl.ds(n * LANES, LANES)], sems.at[n]))
    pool_as_they_come(copies, sizes, held_ref, pooled_ref)
    pack_side(pooled_ref, slice(0, LANES), 0, left_ref)
    pack_side(pooled_ref, slice(LANES, 2 * LANES), 1, right_ref)


def pool_outer_kernel(
    offsets_ref, merit_ref, near_a_ref, near_b_ref, far_a_ref, far_b_ref,
    held_ref, pooled_ref, packed_ref, stage_ref, sems, far_sems,
):
    _, height, width = merit_ref.shape
    blocks = width // LANES
    odd = lax.axis_index("rows") % 2

    def count(v, sign):
        return jnp.maximum(sign * offsets_ref[0, v], 0)

    up, down = 0, 0
    for v in range(VELS):
        up = up + count(v, 1)
        down = down + count(v, -1)

    part = width // 2
    sizes = [(CHUNK, top, part, left) for top in (0, CHUNK) for left in (0, part)]
    copies = []
    for n, (_, top, _, left) in enumerate(sizes):
        rows, cols = pl.ds(top and height - CHUNK, CHUNK), pl.ds(left, part)
        target = held_ref.at[:, pl.ds(top, CHUNK), cols]
        copies.append(pltpu.make_async_copy(merit_ref.at[:, rows, cols], target, sems.at[n]))

    def pack(top, left):
        edge = top // CHUNK
        mine = range(left // LANES, (left + part) // LANES)

        def tile(v, k):
            return pooled_ref[v, edge * CHUNK : (edge + 1) * CHUNK, k * LANES : (k + 1) * LANES].astype(f32)

        if edge == 0:
            at = 0
            for v in range(VELS):
                for k in mine:
                    packed_ref[0, k, pl.ds(at + MAXV, MAXV), :] = tile(v, k)[:MAXV]
                at = at + count(v, -1)
        else:
            at = up
            for v in range(VELS - 1, -1, -1):
                for k in mine:
                    packed_ref[1, k, pl.ds(at, MAXV), :] = tile(v, k)[CHUNK - MAXV :]
                at = at - count(v, 1)

    pool_as_they_come(copies, sizes, held_ref, pooled_ref, pack)

    for slot, ref in enumerate((near_a_ref, near_b_ref)):
        mine = odd if slot == 1 else 1 - odd
        for k in range(blocks):
            piece = packed_ref[mine, k, MAXV : MAXV + SOME_ROWS, :]
            ref[:, k * LANES : (k + 1) * LANES] = piece.astype(bf16)

    @pl.when(jnp.maximum(up, down) > SOME_ROWS)
    def _():
        for slot, ref in enumerate((far_a_ref, far_b_ref)):
            mine = odd if slot == 1 else 1 - odd
            for k in range(blocks):
                piece = packed_ref[mine, k, MAXV + SOME_ROWS : MAXV + ALL_ROWS, :]
                stage_ref[:, k * LANES : (k + 1) * LANES] = piece.astype(bf16)
            copy = pltpu.make_async_copy(stage_ref, ref, far_sems.at[slot])
            copy.start()
            copy.wait()


def pool_cost(merit):
    return pl.CostEstimate(flops=2 * merit.size, bytes_accessed=merit.size, transcendentals=0)


def pool_all(merit, after):
    anywhere = pl.BlockSpec(memory_space=pl.ANY)
    return pl.pallas_call(
        pool_all_kernel,
        out_shape=pltpu.VMEM(merit.shape, bf16),
        in_specs=[anywhere] * (1 + len(after)),
        out_specs=pl.BlockSpec(memory_space=pltpu.VMEM),
        scratch_shapes=[pltpu.VMEM(merit.shape, bf16), pltpu.SemaphoreType.DMA((2 * merit.shape[1] // CHUNK,))],
        cost_estimate=pool_cost(merit),
        compiler_params=params(48 * 2**20),
        name="pool_all",
    )(merit, *after)


def pool_sides(merit, after):
    planes, height, _ = merit.shape
    side = (planes * MAXV // LANES, height, LANES)
    anywhere = pl.BlockSpec(memory_space=pl.ANY)
    return pl.pallas_call(
        pool_sides_kernel,
        out_shape=[jax.ShapeDtypeStruct(side, bf16)] * 2,
        in_specs=[anywhere, anywhere],
        out_specs=[pl.BlockSpec(memory_space=pltpu.VMEM)] * 2,
        scratch_shapes=[pltpu.VMEM((planes, height, 2 * LANES), bf16)] * 2 + [pltpu.SemaphoreType.DMA((2,))],
        cost_estimate=pool_cost(merit),
        compiler_params=params(),
        name="pool_sides",
    )(merit, after)


def pool_outer(merit, offsets):
    planes, height, width = merit.shape
    part = (planes, 2 * CHUNK, width)
    near, far = (SOME_ROWS, width), (ALL_ROWS - SOME_ROWS, width)
    return pl.pallas_call(
        pool_outer_kernel,
        out_shape=[jax.ShapeDtypeStruct(near, bf16)] * 2 + [jax.ShapeDtypeStruct(far, bf16)] * 2,
        in_specs=[smem(), pl.BlockSpec(memory_space=pl.ANY)],
        out_specs=[pl.BlockSpec(memory_space=pltpu.VMEM)] * 2 + [pl.BlockSpec(memory_space=pl.ANY)] * 2,
        scratch_shapes=[
            pltpu.VMEM(part, bf16),
            pltpu.VMEM(part, bf16),
            pltpu.VMEM((2, width // LANES, ALL_ROWS + 2 * MAXV, LANES), f32),
            pltpu.VMEM(far, bf16),
            pltpu.SemaphoreType.DMA((4,)),
            pltpu.SemaphoreType.DMA((2,)),
        ],
        cost_estimate=pool_cost(merit),
        compiler_params=params(),
        name="pool_outer",
    )(offsets, merit)


def weighted_rows(taps_ref, column_ref, k, count):
    half = taps_ref.shape[0] // 2
    total = jnp.zeros((count, LANES), f32)
    for i in range(taps_ref.shape[0]):
        start = MAXV - half + i
        total = total + taps_ref[i] * column_ref[k, start : start + count, :]
    return total


def merge_kernel(
    offsets_ref, taps_ref, pooled_ref, tile_ref, seam_a_ref, seam_b_ref, near_a_ref, near_b_ref,
    west_ref, east_ref, far_a_ref, far_b_ref, far_west_ref, far_east_ref, out_ref,
    halo_ref, side_ref, column_ref, filtered_ref, moved_ref, at_ref, stage_ref, stage_side_ref, sem,
):
    step = pl.program_id(0)
    planes, height, width = out_ref.shape
    blocks = width // LANES
    groups = VELS * MAXV // LANES
    share = LANES // MAXV
    odd = lax.axis_index("rows") % 2
    cuts = [slice(k * LANES, (k + 1) * LANES) for k in range(blocks)]

    @pl.when(step == 0)
    def _():
        up, down = 0, 0
        for v in range(VELS):
            up = up + jnp.maximum(offsets_ref[0, v], 0)
            down = down + jnp.maximum(-offsets_ref[0, v], 0)
        at_ref[0] = 0
        at_ref[1] = 0
        near = slice(MAXV, MAXV + SOME_ROWS)
        start = groups * height
        for e, ref in enumerate((near_a_ref, near_b_ref)):
            for k in range(blocks):
                halo_ref[e, k + 1, near, :] = ref[:, cuts[k]].astype(f32)
            part = slice(start + e * SOME_ROWS, start + (e + 1) * SOME_ROWS)
            halo_ref[e, 0, near, :] = west_ref[part, :].astype(f32)
            halo_ref[e, blocks + 1, near, :] = east_ref[part, :].astype(f32)
        for e, ref in enumerate((west_ref, east_ref)):
            for g in range(groups):
                side_ref[e, g] = ref[g * height : (g + 1) * height, :].astype(f32)
        for k in range(blocks):
            a, b = seam_a_ref[:, cuts[k]], seam_b_ref[:, cuts[k]]
            column_ref[k, :MAXV, :] = jnp.where(odd == 1, a, b)
            column_ref[k, MAXV : MAXV + height, :] = tile_ref[:, cuts[k]]
            column_ref[k, MAXV + height :, :] = jnp.where(odd == 1, b, a)
        for k in range(blocks):
            filtered_ref[k] = weighted_rows(taps_ref, column_ref, k, height)

        @pl.when(jnp.maximum(up, down) > SOME_ROWS)
        def _():
            def bring(source, target):
                copy = pltpu.make_async_copy(source, target, sem)
                copy.start()
                copy.wait()

            far = slice(MAXV + SOME_ROWS, MAXV + ALL_ROWS)
            count = ALL_ROWS - SOME_ROWS
            for e, ref in enumerate((far_a_ref, far_b_ref)):
                bring(ref, stage_ref)
                for k in range(blocks):
                    halo_ref[e, k + 1, far, :] = stage_ref[:, cuts[k]].astype(f32)
            for k, ref in ((0, far_west_ref), (blocks + 1, far_east_ref)):
                bring(ref, stage_side_ref)
                for e in range(2):
                    halo_ref[e, k, far, :] = stage_side_ref[e * count : (e + 1) * count, :].astype(f32)

    def store(p, rows, turn, pieces):
        lane = lax.broadcasted_iota(jnp.int32, pieces[1].shape, 1)
        before = pieces[0]
        for k in range(1, blocks + 2):
            here = pltpu.roll(pieces[k], turn, 1) if k <= blocks else pieces[k]
            moved_ref[p, k - 1, rows, :] = jnp.where(lane < turn, before, here)
            before = here

    moves = []
    up, down = at_ref[0], at_ref[1]
    for p in range(planes):
        v = step * planes + p
        dy, dx = offsets_ref[0, v], offsets_ref[1, v]
        turn = dx & (LANES - 1)
        q = jnp.where(dx >= 0, 0, 1)
        moves.append((dy, q))
        g, w = v // share, v % share
        shift = (dx - (w + 1 - q) * MAXV) & (LANES - 1)
        beyond = pltpu.roll(side_ref[q, g], shift, 1)
        here = [pooled_ref[v, :, cut].astype(f32) for cut in cuts]
        store(p, slice(MAXV, MAXV + height), turn, [beyond] + here + [beyond])
        below = jnp.where(dy >= 0, 0, 1)
        source = pl.ds(jnp.where(dy >= 0, up + dy, down + MAXV), MAXV)
        halo = [halo_ref[below ^ (1 - odd), k, source, :] for k in range(blocks + 2)]
        halo[0] = pltpu.roll(halo[0], turn, 1)
        halo[-1] = pltpu.roll(halo[-1], turn, 1)
        store(p, pl.ds(pl.multiple_of(below * (MAXV + height), MAXV), MAXV), turn, halo)
        up = up + jnp.maximum(dy, 0)
        down = down + jnp.maximum(-dy, 0)
    at_ref[0] = up
    at_ref[1] = down

    for p in range(planes):
        dy, q = moves[p]
        for k in range(blocks):
            shifted = moved_ref[p, k + q, pl.ds(MAXV - dy, height), :]
            out_ref[p, :, cuts[k]] = (filtered_ref[k] + FORGET * shifted).astype(bf16)


def merge(pooled, tile, seams, nears, sides, fars, offsets, taps_col):
    planes, height, width = pooled.shape
    blocks = width // LANES
    groups = planes * MAXV // LANES
    vmem, anywhere = pl.BlockSpec(memory_space=pltpu.VMEM), pl.BlockSpec(memory_space=pl.ANY)
    return pl.pallas_call(
        merge_kernel,
        grid=(planes // SLAB,),
        out_shape=jax.ShapeDtypeStruct((planes, height, width), bf16),
        in_specs=[smem(), smem()] + [vmem] * 8 + [anywhere] * 4,
        out_specs=pl.BlockSpec((SLAB, height, width), lambda i: (i, 0, 0)),
        scratch_shapes=[
            pltpu.VMEM((2, blocks + 2, ALL_ROWS + 2 * MAXV, LANES), f32),
            pltpu.VMEM((2, groups, height, LANES), f32),
            pltpu.VMEM((blocks, height + 2 * MAXV, LANES), f32),
            pltpu.VMEM((blocks, height, LANES), f32),
            pltpu.VMEM((SLAB, blocks + 1, height + 2 * MAXV, LANES), f32),
            pltpu.SMEM((2,), jnp.int32),
            pltpu.VMEM(fars[0].shape, bf16),
            pltpu.VMEM(fars[2].shape, bf16),
            pltpu.SemaphoreType.DMA,
        ],
        compiler_params=params(40 * 2**20),
        name="merge",
    )(offsets, taps_col, pooled, tile, *seams, *nears, *sides, *fars)


def pass_on(value, axis):
    count = lax.axis_size(axis)
    return lax.ppermute(value, axis, [(i, i + 1) for i in range(count - 1)])


def pass_back(value, axis):
    count = lax.axis_size(axis)
    return lax.ppermute(value, axis, [(i + 1, i) for i in range(count - 1)])


def trade(value, axis, first):
    pairs = []
    for i in range(first, lax.axis_size(axis) - 1, 2):
        pairs += [(i, i + 1), (i + 1, i)]
    return lax.ppermute(value, axis, pairs)


def to_sides(right, left, a, b):
    width = a.shape[1]
    east_end, west_end = slice(width - LANES, width), slice(0, LANES)
    last = jnp.concatenate(right + [a[:, east_end], b[:, east_end]], axis=0)
    first = jnp.concatenate(left + [a[:, west_end], b[:, west_end]], axis=0)
    return pass_on(last, "cols"), pass_back(first, "cols")


def far_exchange(far_a, far_b):
    far_b = trade(far_b, "rows", 1)
    far_a = trade(far_a, "rows", 0)
    return (far_a, far_b) + to_sides([], [], far_a, far_b)


def no_exchange(far_a, far_b):
    empty = jnp.zeros((2 * far_a.shape[0], LANES), bf16)
    return far_a, far_b, empty, empty


def on_device(frame, taps_row, taps_col, merit, offsets):
    _, height, width = merit.shape
    turned = offsets.T
    near_a, near_b, far_a, far_b = pool_outer(merit, turned)
    b = trade(near_b, "rows", 1)
    a = trade(near_a, "rows", 0)
    pieces = filter_rows(frame, taps_row, frame.shape[1] // width, far_a)
    tile = lax.all_to_all(pieces, "cols", split_axis=0, concat_axis=0, tiled=True).reshape(height, width)
    shifts = offsets[:, 0]
    most = jnp.maximum(jnp.sum(jnp.maximum(shifts, 0)), jnp.sum(jnp.maximum(-shifts, 0)))
    fars = lax.cond(most > SOME_ROWS, far_exchange, no_exchange, far_a, far_b)
    right, left = pool_sides(merit, pieces)
    west, east = to_sides([right.reshape(-1, LANES)], [left.reshape(-1, LANES)], a, b)
    top, bottom = tile[:MAXV], tile[height - MAXV :]
    odd = lax.axis_index("rows") % 2 == 1
    for_b, for_a = jnp.where(odd, bottom, top), jnp.where(odd, top, bottom)
    seam_b = trade(for_b, "rows", 1)
    seam_a = trade(for_a, "rows", 0)
    pooled = pool_all(merit, (for_a, for_b, fars[2], fars[3]))
    return merge(pooled, tile, (seam_a, seam_b), (a, b), (west, east), fars, turned, taps_col)


def solution(mesh):
    in_specs = (P(("rows", "cols"), None), P(), P(), P(None, "rows", "cols"), P())
    out_specs = P(None, "rows", "cols")
    return jax.shard_map(on_device, mesh=mesh, in_specs=in_specs, out_specs=out_specs, check_vma=False)
```

```python
import functools

import jax
import jax.numpy as jnp
from jax import lax
from jax.experimental import pallas as pl
from jax.experimental.pallas import tpu as pltpu
from jax.sharding import PartitionSpec as P

VGRID = 8
MAXV = 8
VELS = VGRID * VGRID
LANES = 128
FORGET = 0.875
SOME_ROWS = 192
ALL_ROWS = VELS * MAXV
SLAB = 16
CHUNK = 16
LIMIT = 58 * 2**20

f32 = jnp.float32
bf16 = jnp.bfloat16


def params(limit=LIMIT):
    return pltpu.CompilerParams(vmem_limit_bytes=limit)


def brief():
    return pl.CostEstimate(flops=1000, bytes_accessed=1000, transcendentals=0)


def smem():
    return pl.BlockSpec(memory_space=pltpu.SMEM)


def filter_rows_kernel(taps_ref, strip_ref, after_ref, out_ref, pad_ref):
    del after_ref
    half = taps_ref.shape[0] // 2
    height, width = strip_ref.shape
    pad_ref[:, :LANES] = jnp.zeros((height, LANES), f32)
    pad_ref[:, LANES + width :] = jnp.zeros((height, LANES), f32)
    pad_ref[:, LANES : LANES + width] = strip_ref[...]
    count, _, span = out_ref.shape
    for piece in range(count):
        start = LANES + piece * span
        total = jnp.zeros((height, span), f32)
        for j in range(taps_ref.shape[0]):
            total = total + taps_ref[j] * pad_ref[:, start + j - half : start + j - half + span]
        out_ref[piece] = total


def filter_rows(strip, taps_row, pieces, after):
    height, width = strip.shape
    return pl.pallas_call(
        filter_rows_kernel,
        out_shape=jax.ShapeDtypeStruct((pieces, height, width // pieces), f32),
        in_specs=[smem(), pl.BlockSpec(memory_space=pltpu.VMEM), pl.BlockSpec(memory_space=pl.ANY)],
        out_specs=pl.BlockSpec(memory_space=pltpu.VMEM),
        scratch_shapes=[pltpu.VMEM((height, width + 2 * LANES), f32)],
        cost_estimate=brief(),
        compiler_params=params(16 * 2**20),
        name="filter_rows",
    )(taps_row, strip, after)


def max_of_three(values):
    total = len(values)
    pairs = [jnp.maximum(values[i], values[i + 1]) for i in range(total - 1)]
    middle = [jnp.maximum(pairs[i - 1], values[i + 1]) for i in range(1, total - 1)]
    return [pairs[0]] + middle + [pairs[-1]]


def pool_chunk(merit_ref, pooled_ref, rows, cols):
    def line(a):
        return max_of_three([merit_ref[a * VGRID + b, rows, cols] for b in range(VGRID)])

    def emit(a, planes):
        for b in range(VGRID):
            pooled_ref[a * VGRID + b, rows, cols] = planes[b]

    last, here = line(0), line(1)
    pair = [jnp.maximum(x, y) for x, y in zip(last, here)]
    emit(0, pair)
    for a in range(2, VGRID):
        after = line(a)
        emit(a - 1, [jnp.maximum(x, y) for x, y in zip(pair, after)])
        pair = [jnp.maximum(x, y) for x, y in zip(here, after)]
        here = after
    emit(VGRID - 1, pair)


def pack_side(pooled_ref, cols, turn, target_ref):
    height = pooled_ref.shape[1]
    lane_group = lax.broadcasted_iota(jnp.int32, (height, LANES), 1) // MAXV
    share = LANES // MAXV
    for g in range(VELS // share):
        total = jnp.zeros((height, LANES), f32)
        for w in range(share):
            edge = pooled_ref[g * share + w, :, cols].astype(f32)
            total = jnp.where(lane_group == w, pltpu.roll(edge, (w + turn) * MAXV % LANES, 1), total)
        target_ref[g] = total.astype(bf16)


def pool_as_they_come(copies, sizes, held_ref, pooled_ref, then=None):
    for copy in copies:
        copy.start()
    for copy, (height, top, width, left) in zip(copies, sizes):
        copy.wait()
        across = width // LANES

        def one(i, carry):
            rows = pl.ds(pl.multiple_of(top + i // across * CHUNK, CHUNK), CHUNK)
            cols = pl.ds(pl.multiple_of(left + i % across * LANES, LANES), LANES)
            pool_chunk(held_ref, pooled_ref, rows, cols)
            return carry

        lax.fori_loop(0, height // CHUNK * across, one, 0)
        if then is not None:
            then(top, left)


def pool_all_kernel(merit_ref, *refs):
    pooled_ref, held_ref, sems = refs[-3:]
    _, height, width = merit_ref.shape
    part = width // 2
    sizes = [(CHUNK, top, part, left) for top in range(0, height, CHUNK) for left in (0, part)]
    copies = []
    for n, (_, top, _, left) in enumerate(sizes):
        at = (slice(None), pl.ds(top, CHUNK), pl.ds(left, part))
        copies.append(pltpu.make_async_copy(merit_ref.at[at], held_ref.at[at], sems.at[n]))
    pool_as_they_come(copies, sizes, held_ref, pooled_ref)


def pool_sides_kernel(merit_ref, after_ref, right_ref, left_ref, held_ref, pooled_ref, sems):
    del after_ref
    _, height, width = merit_ref.shape
    sizes = [(height, 0, LANES, left) for left in (0, LANES)]
    copies = []
    for n, first in enumerate((0, width - LANES)):
        source = merit_ref.at[:, :, pl.ds(first, LANES)]
        copies.append(pltpu.make_async_copy(source, held_ref.at[:, :, pl.ds(n * LANES, LANES)], sems.at[n]))
    pool_as_they_come(copies, sizes, held_ref, pooled_ref)
    pack_side(pooled_ref, slice(0, LANES), 0, left_ref)
    pack_side(pooled_ref, slice(LANES, 2 * LANES), 1, right_ref)


def pool_outer_kernel(
    offsets_ref, merit_ref, near_a_ref, near_b_ref, far_a_ref, far_b_ref, far_west_ref, far_east_ref, more_ref,
    held_ref, pooled_ref, packed_ref, stage_ref, sems, far_sems,
):
    del far_west_ref, far_east_ref
    _, height, width = merit_ref.shape
    blocks = width // LANES
    odd = lax.axis_index("rows") % 2

    def count(v, sign):
        return jnp.maximum(sign * offsets_ref[0, v], 0)

    up, down = 0, 0
    for v in range(VELS):
        up = up + count(v, 1)
        down = down + count(v, -1)

    part = width // 2
    sizes = [(CHUNK, top, part, left) for top in (0, CHUNK) for left in (0, part)]
    copies = []
    for n, (_, top, _, left) in enumerate(sizes):
        rows, cols = pl.ds(top and height - CHUNK, CHUNK), pl.ds(left, part)
        target = held_ref.at[:, pl.ds(top, CHUNK), cols]
        copies.append(pltpu.make_async_copy(merit_ref.at[:, rows, cols], target, sems.at[n]))

    def pack(top, left):
        edge = top // CHUNK
        mine = range(left // LANES, (left + part) // LANES)

        def tile(v, k):
            return pooled_ref[v, edge * CHUNK : (edge + 1) * CHUNK, k * LANES : (k + 1) * LANES].astype(f32)

        if edge == 0:
            at = 0
            for v in range(VELS):
                for k in mine:
                    packed_ref[0, k, pl.ds(at + MAXV, MAXV), :] = tile(v, k)[:MAXV]
                at = at + count(v, -1)
        else:
            at = up
            for v in range(VELS - 1, -1, -1):
                for k in mine:
                    packed_ref[1, k, pl.ds(at, MAXV), :] = tile(v, k)[CHUNK - MAXV :]
                at = at - count(v, 1)

    pool_as_they_come(copies, sizes, held_ref, pooled_ref, pack)

    for slot, ref in enumerate((near_a_ref, near_b_ref)):
        mine = odd if slot == 1 else 1 - odd
        for k in range(blocks):
            piece = packed_ref[mine, k, MAXV : MAXV + SOME_ROWS, :]
            ref[:, k * LANES : (k + 1) * LANES] = piece.astype(bf16)

    more = jnp.maximum(up, down) > SOME_ROWS
    more_ref[0] = more.astype(jnp.int32)

    @pl.when(more)
    def _():
        for slot, ref in enumerate((far_a_ref, far_b_ref)):
            mine = odd if slot == 1 else 1 - odd
            for k in range(blocks):
                piece = packed_ref[mine, k, MAXV + SOME_ROWS : MAXV + ALL_ROWS, :]
                stage_ref[:, k * LANES : (k + 1) * LANES] = piece.astype(bf16)
            copy = pltpu.make_async_copy(stage_ref, ref, far_sems.at[slot])
            copy.start()
            copy.wait()


def pool_cost(merit):
    return pl.CostEstimate(flops=2 * merit.size, bytes_accessed=merit.size, transcendentals=0)


def pool_all(merit, after):
    anywhere = pl.BlockSpec(memory_space=pl.ANY)
    return pl.pallas_call(
        pool_all_kernel,
        out_shape=pltpu.VMEM(merit.shape, bf16),
        in_specs=[anywhere] + [pl.BlockSpec(memory_space=pltpu.VMEM)] * 2 + [anywhere] * 2,
        out_specs=pl.BlockSpec(memory_space=pltpu.VMEM),
        scratch_shapes=[pltpu.VMEM(merit.shape, bf16), pltpu.SemaphoreType.DMA((2 * merit.shape[1] // CHUNK,))],
        cost_estimate=pool_cost(merit),
        compiler_params=params(48 * 2**20),
        name="pool_all",
    )(merit, *after)


def pool_sides(merit, after):
    planes, height, _ = merit.shape
    side = (planes * MAXV // LANES, height, LANES)
    anywhere = pl.BlockSpec(memory_space=pl.ANY)
    return pl.pallas_call(
        pool_sides_kernel,
        out_shape=[pltpu.VMEM(side, bf16)] * 2,
        in_specs=[anywhere, anywhere],
        out_specs=[pl.BlockSpec(memory_space=pltpu.VMEM)] * 2,
        scratch_shapes=[pltpu.VMEM((planes, height, 2 * LANES), bf16)] * 2 + [pltpu.SemaphoreType.DMA((2,))],
        cost_estimate=brief(),
        compiler_params=params(),
        name="pool_sides",
    )(merit, after)


def pool_outer(merit, offsets):
    planes, height, width = merit.shape
    part = (planes, 2 * CHUNK, width)
    near, far = (SOME_ROWS, width), (ALL_ROWS - SOME_ROWS, width)
    return pl.pallas_call(
        pool_outer_kernel,
        out_shape=[jax.ShapeDtypeStruct(near, bf16)] * 2
        + [pltpu.HBM(far, bf16)] * 2
        + [pltpu.HBM((2 * far[0], LANES), bf16)] * 2
        + [jax.ShapeDtypeStruct((1,), jnp.int32)],
        in_specs=[smem(), pl.BlockSpec(memory_space=pl.ANY)],
        out_specs=[pl.BlockSpec(memory_space=pltpu.VMEM)] * 2 + [pl.BlockSpec(memory_space=pl.ANY)] * 4 + [smem()],
        scratch_shapes=[
            pltpu.VMEM(part, bf16),
            pltpu.VMEM(part, bf16),
            pltpu.VMEM((2, width // LANES, ALL_ROWS + 2 * MAXV, LANES), f32),
            pltpu.VMEM(far, bf16),
            pltpu.SemaphoreType.DMA((4,)),
            pltpu.SemaphoreType.DMA((2,)),
        ],
        cost_estimate=pool_cost(merit),
        compiler_params=params(),
        name="pool_outer",
    )(offsets, merit)


def join_kernel(right_ref, left_ref, a_ref, b_ref, last_ref, first_ref):
    groups, height, _ = right_ref.shape
    width = a_ref.shape[1]
    for side, out, edge in ((right_ref, last_ref, width - LANES), (left_ref, first_ref, 0)):
        for g in range(groups):
            out[g * height : (g + 1) * height, :] = side[g]
        for e, ref in enumerate((a_ref, b_ref)):
            start = groups * height + e * SOME_ROWS
            out[start : start + SOME_ROWS, :] = ref[:, edge : edge + LANES]


def join(right, left, a, b):
    groups, height, _ = right.shape
    vmem = pl.BlockSpec(memory_space=pltpu.VMEM)
    return pl.pallas_call(
        join_kernel,
        out_shape=[jax.ShapeDtypeStruct((groups * height + 2 * SOME_ROWS, LANES), bf16)] * 2,
        in_specs=[vmem] * 4,
        out_specs=[vmem] * 2,
        cost_estimate=brief(),
        compiler_params=params(16 * 2**20),
        name="join",
    )(right, left, a, b)


def weighted_rows(taps_ref, column_ref, k, count):
    half = taps_ref.shape[0] // 2
    total = jnp.zeros((count, LANES), f32)
    for i in range(taps_ref.shape[0]):
        start = MAXV - half + i
        total = total + taps_ref[i] * column_ref[k, start : start + count, :]
    return total


def merge_kernel(
    offsets_ref, taps_ref, pooled_ref, tile_ref, seam_a_ref, seam_b_ref, near_a_ref, near_b_ref,
    west_ref, east_ref, far_a_ref, far_b_ref, far_west_ref, far_east_ref, out_ref,
    halo_ref, side_ref, column_ref, filtered_ref, moved_ref, at_ref, stage_ref, stage_side_ref, sem,
):
    step = pl.program_id(0)
    planes, height, width = out_ref.shape
    blocks = width // LANES
    groups = VELS * MAXV // LANES
    share = LANES // MAXV
    odd = lax.axis_index("rows") % 2
    cuts = [slice(k * LANES, (k + 1) * LANES) for k in range(blocks)]

    @pl.when(step == 0)
    def _():
        up, down = 0, 0
        for v in range(VELS):
            up = up + jnp.maximum(offsets_ref[0, v], 0)
            down = down + jnp.maximum(-offsets_ref[0, v], 0)
        at_ref[0] = 0
        at_ref[1] = 0
        near = slice(MAXV, MAXV + SOME_ROWS)
        start = groups * height
        for e, ref in enumerate((near_a_ref, near_b_ref)):
            for k in range(blocks):
                halo_ref[e, k + 1, near, :] = ref[:, cuts[k]].astype(f32)
            part = slice(start + e * SOME_ROWS, start + (e + 1) * SOME_ROWS)
            halo_ref[e, 0, near, :] = west_ref[part, :].astype(f32)
            halo_ref[e, blocks + 1, near, :] = east_ref[part, :].astype(f32)
        for e, ref in enumerate((west_ref, east_ref)):
            for g in range(groups):
                side_ref[e, g] = ref[g * height : (g + 1) * height, :].astype(f32)
        for k in range(blocks):
            a, b = seam_a_ref[:, cuts[k]], seam_b_ref[:, cuts[k]]
            column_ref[k, :MAXV, :] = jnp.where(odd == 1, a, b)
            column_ref[k, MAXV : MAXV + height, :] = tile_ref[:, cuts[k]]
            column_ref[k, MAXV + height :, :] = jnp.where(odd == 1, b, a)
        for k in range(blocks):
            filtered_ref[k] = weighted_rows(taps_ref, column_ref, k, height)

        @pl.when(jnp.maximum(up, down) > SOME_ROWS)
        def _():
            def bring(source, target):
                copy = pltpu.make_async_copy(source, target, sem)
                copy.start()
                copy.wait()

            far = slice(MAXV + SOME_ROWS, MAXV + ALL_ROWS)
            count = ALL_ROWS - SOME_ROWS
            for e, ref in enumerate((far_a_ref, far_b_ref)):
                bring(ref, stage_ref)
                for k in range(blocks):
                    halo_ref[e, k + 1, far, :] = stage_ref[:, cuts[k]].astype(f32)
            for k, ref in ((0, far_west_ref), (blocks + 1, far_east_ref)):
                bring(ref, stage_side_ref)
                for e in range(2):
                    halo_ref[e, k, far, :] = stage_side_ref[e * count : (e + 1) * count, :].astype(f32)

    def store(p, rows, turn, pieces):
        lane = lax.broadcasted_iota(jnp.int32, pieces[1].shape, 1)
        before = pieces[0]
        for k in range(1, blocks + 2):
            here = pltpu.roll(pieces[k], turn, 1) if k <= blocks else pieces[k]
            moved_ref[p, k - 1, rows, :] = jnp.where(lane < turn, before, here)
            before = here

    moves = []
    up, down = at_ref[0], at_ref[1]
    for p in range(planes):
        v = step * planes + p
        dy, dx = offsets_ref[0, v], offsets_ref[1, v]
        turn = dx & (LANES - 1)
        q = jnp.where(dx >= 0, 0, 1)
        moves.append((dy, q))
        g, w = v // share, v % share
        shift = (dx - (w + 1 - q) * MAXV) & (LANES - 1)
        beyond = pltpu.roll(side_ref[q, g], shift, 1)
        here = [pooled_ref[v, :, cut].astype(f32) for cut in cuts]
        store(p, slice(MAXV, MAXV + height), turn, [beyond] + here + [beyond])
        below = jnp.where(dy >= 0, 0, 1)
        source = pl.ds(jnp.where(dy >= 0, up + dy, down + MAXV), MAXV)
        halo = [halo_ref[below ^ (1 - odd), k, source, :] for k in range(blocks + 2)]
        halo[0] = pltpu.roll(halo[0], turn, 1)
        halo[-1] = pltpu.roll(halo[-1], turn, 1)
        store(p, pl.ds(pl.multiple_of(below * (MAXV + height), MAXV), MAXV), turn, halo)
        up = up + jnp.maximum(dy, 0)
        down = down + jnp.maximum(-dy, 0)
    at_ref[0] = up
    at_ref[1] = down

    for p in range(planes):
        dy, q = moves[p]
        for k in range(blocks):
            shifted = moved_ref[p, k + q, pl.ds(MAXV - dy, height), :]
            out_ref[p, :, cuts[k]] = (filtered_ref[k] + FORGET * shifted).astype(bf16)


def merge(pooled, tile, seams, nears, sides, fars, offsets, taps_col):
    planes, height, width = pooled.shape
    blocks = width // LANES
    groups = planes * MAXV // LANES
    vmem, anywhere = pl.BlockSpec(memory_space=pltpu.VMEM), pl.BlockSpec(memory_space=pl.ANY)
    return pl.pallas_call(
        merge_kernel,
        grid=(planes // SLAB,),
        out_shape=jax.ShapeDtypeStruct((planes, height, width), bf16),
        in_specs=[smem(), smem()] + [vmem] * 8 + [anywhere] * 4,
        out_specs=pl.BlockSpec((SLAB, height, width), lambda i: (i, 0, 0)),
        scratch_shapes=[
            pltpu.VMEM((2, blocks + 2, ALL_ROWS + 2 * MAXV, LANES), f32),
            pltpu.VMEM((2, groups, height, LANES), f32),
            pltpu.VMEM((blocks, height + 2 * MAXV, LANES), f32),
            pltpu.VMEM((blocks, height, LANES), f32),
            pltpu.VMEM((SLAB, blocks + 1, height + 2 * MAXV, LANES), f32),
            pltpu.SMEM((2,), jnp.int32),
            pltpu.VMEM(fars[0].shape, bf16),
            pltpu.VMEM(fars[2].shape, bf16),
            pltpu.SemaphoreType.DMA,
        ],
        compiler_params=params(40 * 2**20),
        name="merge",
    )(offsets, taps_col, pooled, tile, *seams, *nears, *sides, *fars)


def pass_on(value, axis):
    count = lax.axis_size(axis)
    return lax.ppermute(value, axis, [(i, i + 1) for i in range(count - 1)])


def pass_back(value, axis):
    count = lax.axis_size(axis)
    return lax.ppermute(value, axis, [(i + 1, i) for i in range(count - 1)])


def trade(value, axis, first):
    pairs = []
    for i in range(first, lax.axis_size(axis) - 1, 2):
        pairs += [(i, i + 1), (i + 1, i)]
    return lax.ppermute(value, axis, pairs)


def far_exchange(state):
    count, far_a, far_b, _, _ = state
    far_b = trade(far_b, "rows", 1)
    far_a = trade(far_a, "rows", 0)
    width = far_a.shape[1]
    last = jnp.concatenate([far_a[:, width - LANES :], far_b[:, width - LANES :]], axis=0)
    first = jnp.concatenate([far_a[:, :LANES], far_b[:, :LANES]], axis=0)
    return count - 1, far_a, far_b, pass_on(last, "cols"), pass_back(first, "cols")


def on_device(frame, taps_row, taps_col, merit, offsets):
    _, height, width = merit.shape
    turned = offsets.T
    near_a, near_b, *fars, more = pool_outer(merit, turned)
    b = trade(near_b, "rows", 1)
    a = trade(near_a, "rows", 0)
    pieces = filter_rows(frame, taps_row, frame.shape[1] // width, a)
    tile = lax.all_to_all(pieces, "cols", split_axis=0, concat_axis=0, tiled=True).reshape(height, width)
    _, *fars = lax.while_loop(lambda state: state[0] > 0, far_exchange, (more.reshape(()), *fars))
    right, left = pool_sides(merit, pieces)
    last, first = join(right, left, a, b)
    west, east = pass_on(last, "cols"), pass_back(first, "cols")
    top, bottom = tile[:MAXV], tile[height - MAXV :]
    odd = lax.axis_index("rows") % 2 == 1
    for_b, for_a = jnp.where(odd, bottom, top), jnp.where(odd, top, bottom)
    seam_b = trade(for_b, "rows", 1)
    seam_a = trade(for_a, "rows", 0)
    pooled = pool_all(merit, (for_a, for_b, fars[2], fars[3]))
    return merge(pooled, tile, (seam_a, seam_b), (a, b), (west, east), fars, turned, taps_col)


def solution(mesh):
    in_specs = (P(("rows", "cols"), None), P(), P(), P(None, "rows", "cols"), P())
    out_specs = P(None, "rows", "cols")
    return jax.shard_map(on_device, mesh=mesh, in_specs=in_specs, out_specs=out_specs, check_vma=False)
```

```python
import functools

import jax
import jax.numpy as jnp
from jax import lax
from jax.experimental import pallas as pl
from jax.experimental.pallas import tpu as pltpu
from jax.sharding import PartitionSpec as P

VGRID = 8
MAXV = 8
VELS = VGRID * VGRID
LANES = 128
FORGET = 0.875
SOME_ROWS = 208
ALL_ROWS = VELS * MAXV
SLAB = 16
CHUNK = 16
LIMIT = 58 * 2**20

f32 = jnp.float32
bf16 = jnp.bfloat16


def params(limit=LIMIT):
    return pltpu.CompilerParams(vmem_limit_bytes=limit)


def brief():
    return pl.CostEstimate(flops=1000, bytes_accessed=1000, transcendentals=0)


def smem():
    return pl.BlockSpec(memory_space=pltpu.SMEM)


def filter_rows_kernel(taps_ref, strip_ref, after_ref, out_ref, pad_ref):
    del after_ref
    half = taps_ref.shape[0] // 2
    height, width = strip_ref.shape
    pad_ref[:, :LANES] = jnp.zeros((height, LANES), f32)
    pad_ref[:, LANES + width :] = jnp.zeros((height, LANES), f32)
    pad_ref[:, LANES : LANES + width] = strip_ref[...]
    count, _, span = out_ref.shape
    for piece in range(count):
        start = LANES + piece * span
        total = jnp.zeros((height, span), f32)
        for j in range(taps_ref.shape[0]):
            total = total + taps_ref[j] * pad_ref[:, start + j - half : start + j - half + span]
        out_ref[piece] = total


def filter_rows(strip, taps_row, pieces, after):
    height, width = strip.shape
    return pl.pallas_call(
        filter_rows_kernel,
        out_shape=jax.ShapeDtypeStruct((pieces, height, width // pieces), f32),
        in_specs=[smem(), pl.BlockSpec(memory_space=pltpu.VMEM), pl.BlockSpec(memory_space=pl.ANY)],
        out_specs=pl.BlockSpec(memory_space=pltpu.VMEM),
        scratch_shapes=[pltpu.VMEM((height, width + 2 * LANES), f32)],
        cost_estimate=brief(),
        compiler_params=params(16 * 2**20),
        name="filter_rows",
    )(taps_row, strip, after)


def max_of_three(values):
    total = len(values)
    pairs = [jnp.maximum(values[i], values[i + 1]) for i in range(total - 1)]
    middle = [jnp.maximum(pairs[i - 1], values[i + 1]) for i in range(1, total - 1)]
    return [pairs[0]] + middle + [pairs[-1]]


def pool_chunk(merit_ref, pooled_ref, rows, cols):
    def line(a):
        return max_of_three([merit_ref[a * VGRID + b, rows, cols] for b in range(VGRID)])

    def emit(a, planes):
        for b in range(VGRID):
            pooled_ref[a * VGRID + b, rows, cols] = planes[b]

    last, here = line(0), line(1)
    pair = [jnp.maximum(x, y) for x, y in zip(last, here)]
    emit(0, pair)
    for a in range(2, VGRID):
        after = line(a)
        emit(a - 1, [jnp.maximum(x, y) for x, y in zip(pair, after)])
        pair = [jnp.maximum(x, y) for x, y in zip(here, after)]
        here = after
    emit(VGRID - 1, pair)


def pack_side(pooled_ref, cols, turn, target_ref):
    height = pooled_ref.shape[1]
    lane_group = lax.broadcasted_iota(jnp.int32, (height, LANES), 1) // MAXV
    share = LANES // MAXV
    for g in range(VELS // share):
        total = jnp.zeros((height, LANES), f32)
        for w in range(share):
            edge = pooled_ref[g * share + w, :, cols].astype(f32)
            total = jnp.where(lane_group == w, pltpu.roll(edge, (w + turn) * MAXV % LANES, 1), total)
        target_ref[g] = total.astype(bf16)


def pool_as_they_come(copies, sizes, held_ref, pooled_ref, then=None):
    for copy in copies:
        copy.start()
    for copy, (height, top, width, left) in zip(copies, sizes):
        copy.wait()
        across = width // LANES

        def one(i, carry):
            rows = pl.ds(pl.multiple_of(top + i // across * CHUNK, CHUNK), CHUNK)
            cols = pl.ds(pl.multiple_of(left + i % across * LANES, LANES), LANES)
            pool_chunk(held_ref, pooled_ref, rows, cols)
            return carry

        lax.fori_loop(0, height // CHUNK * across, one, 0)
        if then is not None:
            then(top, left)


def pool_all_kernel(merit_ref, *refs):
    pooled_ref, held_ref, sems = refs[-3:]
    _, height, width = merit_ref.shape
    part = width // 2
    sizes = [(CHUNK, top, part, left) for top in range(0, height, CHUNK) for left in (0, part)]
    copies = []
    for n, (_, top, _, left) in enumerate(sizes):
        at = (slice(None), pl.ds(top, CHUNK), pl.ds(left, part))
        copies.append(pltpu.make_async_copy(merit_ref.at[at], held_ref.at[at], sems.at[n]))
    pool_as_they_come(copies, sizes, held_ref, pooled_ref)


def pool_sides_kernel(merit_ref, after_ref, far_ref, right_ref, left_ref, held_ref, pooled_ref, sems):
    del after_ref, far_ref
    _, height, width = merit_ref.shape
    sizes = [(height, 0, LANES, left) for left in (0, LANES)]
    copies = []
    for n, first in enumerate((0, width - LANES)):
        source = merit_ref.at[:, :, pl.ds(first, LANES)]
        copies.append(pltpu.make_async_copy(source, held_ref.at[:, :, pl.ds(n * LANES, LANES)], sems.at[n]))
    pool_as_they_come(copies, sizes, held_ref, pooled_ref)
    pack_side(pooled_ref, slice(0, LANES), 0, left_ref)
    pack_side(pooled_ref, slice(LANES, 2 * LANES), 1, right_ref)


def pool_outer_kernel(
    offsets_ref, merit_ref, near_a_ref, near_b_ref, far_a_ref, far_b_ref, far_west_ref, far_east_ref, more_ref,
    held_ref, pooled_ref, packed_ref, stage_ref, sems, far_sems,
):
    del far_west_ref, far_east_ref
    _, height, width = merit_ref.shape
    blocks = width // LANES
    odd = lax.axis_index("rows") % 2

    def count(v, sign):
        return jnp.maximum(sign * offsets_ref[0, v], 0)

    up, down = 0, 0
    for v in range(VELS):
        up = up + count(v, 1)
        down = down + count(v, -1)

    part = width // 2
    sizes = [(CHUNK, top, part, left) for top in (0, CHUNK) for left in (0, part)]
    copies = []
    for n, (_, top, _, left) in enumerate(sizes):
        rows, cols = pl.ds(top and height - CHUNK, CHUNK), pl.ds(left, part)
        target = held_ref.at[:, pl.ds(top, CHUNK), cols]
        copies.append(pltpu.make_async_copy(merit_ref.at[:, rows, cols], target, sems.at[n]))

    def pack(top, left):
        edge = top // CHUNK
        mine = range(left // LANES, (left + part) // LANES)

        def tile(v, k):
            return pooled_ref[v, edge * CHUNK : (edge + 1) * CHUNK, k * LANES : (k + 1) * LANES].astype(f32)

        if edge == 0:
            at = 0
            for v in range(VELS):
                for k in mine:
                    packed_ref[0, k, pl.ds(at + MAXV, MAXV), :] = tile(v, k)[:MAXV]
                at = at + count(v, -1)
        else:
            at = up
            for v in range(VELS - 1, -1, -1):
                for k in mine:
                    packed_ref[1, k, pl.ds(at, MAXV), :] = tile(v, k)[CHUNK - MAXV :]
                at = at - count(v, 1)

    pool_as_they_come(copies, sizes, held_ref, pooled_ref, pack)

    for slot, ref in enumerate((near_a_ref, near_b_ref)):
        mine = odd if slot == 1 else 1 - odd
        for k in range(blocks):
            piece = packed_ref[mine, k, MAXV : MAXV + SOME_ROWS, :]
            ref[:, k * LANES : (k + 1) * LANES] = piece.astype(bf16)

    more = jnp.maximum(up, down) > SOME_ROWS
    more_ref[0] = more.astype(jnp.int32)

    @pl.when(more)
    def _():
        for slot, ref in enumerate((far_a_ref, far_b_ref)):
            mine = odd if slot == 1 else 1 - odd
            for k in range(blocks):
                piece = packed_ref[mine, k, MAXV + SOME_ROWS : MAXV + ALL_ROWS, :]
                stage_ref[:, k * LANES : (k + 1) * LANES] = piece.astype(bf16)
            copy = pltpu.make_async_copy(stage_ref, ref, far_sems.at[slot])
            copy.start()
            copy.wait()


def pool_cost(merit):
    return pl.CostEstimate(flops=2 * merit.size, bytes_accessed=merit.size, transcendentals=0)


def pool_all(merit, after):
    anywhere = pl.BlockSpec(memory_space=pl.ANY)
    return pl.pallas_call(
        pool_all_kernel,
        out_shape=pltpu.VMEM(merit.shape, bf16),
        in_specs=[anywhere] * (1 + len(after)),
        out_specs=pl.BlockSpec(memory_space=pltpu.VMEM),
        scratch_shapes=[pltpu.VMEM(merit.shape, bf16), pltpu.SemaphoreType.DMA((2 * merit.shape[1] // CHUNK,))],
        cost_estimate=pool_cost(merit),
        compiler_params=params(48 * 2**20),
        name="pool_all",
    )(merit, *after)


def pool_sides(merit, after, far):
    planes, height, _ = merit.shape
    side = (planes * MAXV // LANES, height, LANES)
    anywhere = pl.BlockSpec(memory_space=pl.ANY)
    return pl.pallas_call(
        pool_sides_kernel,
        out_shape=[pltpu.VMEM(side, bf16)] * 2,
        in_specs=[anywhere] * 3,
        out_specs=[pl.BlockSpec(memory_space=pltpu.VMEM)] * 2,
        scratch_shapes=[pltpu.VMEM((planes, height, 2 * LANES), bf16)] * 2 + [pltpu.SemaphoreType.DMA((2,))],
        cost_estimate=brief(),
        compiler_params=params(),
        name="pool_sides",
    )(merit, after, far)


def pool_outer(merit, offsets):
    planes, height, width = merit.shape
    part = (planes, 2 * CHUNK, width)
    near, far = (SOME_ROWS, width), (ALL_ROWS - SOME_ROWS, width)
    return pl.pallas_call(
        pool_outer_kernel,
        out_shape=[jax.ShapeDtypeStruct(near, bf16)] * 2
        + [pltpu.HBM(far, bf16)] * 2
        + [pltpu.HBM((2 * far[0], LANES), bf16)] * 2
        + [jax.ShapeDtypeStruct((1,), jnp.int32)],
        in_specs=[smem(), pl.BlockSpec(memory_space=pl.ANY)],
        out_specs=[pl.BlockSpec(memory_space=pltpu.VMEM)] * 2 + [pl.BlockSpec(memory_space=pl.ANY)] * 4 + [smem()],
        scratch_shapes=[
            pltpu.VMEM(part, bf16),
            pltpu.VMEM(part, bf16),
            pltpu.VMEM((2, width // LANES, ALL_ROWS + 2 * MAXV, LANES), f32),
            pltpu.VMEM(far, bf16),
            pltpu.SemaphoreType.DMA((4,)),
            pltpu.SemaphoreType.DMA((2,)),
        ],
        cost_estimate=pool_cost(merit),
        compiler_params=params(),
        name="pool_outer",
    )(offsets, merit)


def join_kernel(right_ref, left_ref, a_ref, b_ref, last_ref, first_ref):
    groups, height, _ = right_ref.shape
    width = a_ref.shape[1]
    for side, out, edge in ((right_ref, last_ref, width - LANES), (left_ref, first_ref, 0)):
        for g in range(groups):
            out[g * height : (g + 1) * height, :] = side[g]
        for e, ref in enumerate((a_ref, b_ref)):
            start = groups * height + e * SOME_ROWS
            out[start : start + SOME_ROWS, :] = ref[:, edge : edge + LANES]


def join(right, left, a, b):
    groups, height, _ = right.shape
    vmem = pl.BlockSpec(memory_space=pltpu.VMEM)
    return pl.pallas_call(
        join_kernel,
        out_shape=[jax.ShapeDtypeStruct((groups * height + 2 * SOME_ROWS, LANES), bf16)] * 2,
        in_specs=[vmem] * 4,
        out_specs=[vmem] * 2,
        cost_estimate=brief(),
        compiler_params=params(16 * 2**20),
        name="join",
    )(right, left, a, b)


def weighted_rows(taps_ref, column_ref, k, count):
    half = taps_ref.shape[0] // 2
    total = jnp.zeros((count, LANES), f32)
    for i in range(taps_ref.shape[0]):
        start = MAXV - half + i
        total = total + taps_ref[i] * column_ref[k, start : start + count, :]
    return total


def merge_kernel(
    offsets_ref, taps_ref, pooled_ref, tile_ref, seam_a_ref, seam_b_ref, near_a_ref, near_b_ref,
    west_ref, east_ref, far_a_ref, far_b_ref, far_west_ref, far_east_ref, out_ref,
    halo_ref, side_ref, column_ref, filtered_ref, moved_ref, at_ref, stage_ref, stage_side_ref, sem,
):
    step = pl.program_id(0)
    planes, height, width = out_ref.shape
    blocks = width // LANES
    groups = VELS * MAXV // LANES
    share = LANES // MAXV
    odd = lax.axis_index("rows") % 2
    cuts = [slice(k * LANES, (k + 1) * LANES) for k in range(blocks)]

    @pl.when(step == 0)
    def _():
        up, down = 0, 0
        for v in range(VELS):
            up = up + jnp.maximum(offsets_ref[0, v], 0)
            down = down + jnp.maximum(-offsets_ref[0, v], 0)
        at_ref[0] = 0
        at_ref[1] = 0
        near = slice(MAXV, MAXV + SOME_ROWS)
        start = groups * height
        for e, ref in enumerate((near_a_ref, near_b_ref)):
            for k in range(blocks):
                halo_ref[e, k + 1, near, :] = ref[:, cuts[k]].astype(f32)
            part = slice(start + e * SOME_ROWS, start + (e + 1) * SOME_ROWS)
            halo_ref[e, 0, near, :] = west_ref[part, :].astype(f32)
            halo_ref[e, blocks + 1, near, :] = east_ref[part, :].astype(f32)
        for e, ref in enumerate((west_ref, east_ref)):
            for g in range(groups):
                side_ref[e, g] = ref[g * height : (g + 1) * height, :].astype(f32)
        for k in range(blocks):
            a, b = seam_a_ref[:, cuts[k]], seam_b_ref[:, cuts[k]]
            column_ref[k, :MAXV, :] = jnp.where(odd == 1, a, b)
            column_ref[k, MAXV : MAXV + height, :] = tile_ref[:, cuts[k]]
            column_ref[k, MAXV + height :, :] = jnp.where(odd == 1, b, a)
        for k in range(blocks):
            filtered_ref[k] = weighted_rows(taps_ref, column_ref, k, height)

        @pl.when(jnp.maximum(up, down) > SOME_ROWS)
        def _():
            def bring(source, target):
                copy = pltpu.make_async_copy(source, target, sem)
                copy.start()
                copy.wait()

            far = slice(MAXV + SOME_ROWS, MAXV + ALL_ROWS)
            count = ALL_ROWS - SOME_ROWS
            for e, ref in enumerate((far_a_ref, far_b_ref)):
                bring(ref, stage_ref)
                for k in range(blocks):
                    halo_ref[e, k + 1, far, :] = stage_ref[:, cuts[k]].astype(f32)
            for k, ref in ((0, far_west_ref), (blocks + 1, far_east_ref)):
                bring(ref, stage_side_ref)
                for e in range(2):
                    halo_ref[e, k, far, :] = stage_side_ref[e * count : (e + 1) * count, :].astype(f32)

    def store(p, rows, turn, pieces):
        lane = lax.broadcasted_iota(jnp.int32, pieces[1].shape, 1)
        before = pieces[0]
        for k in range(1, blocks + 2):
            here = pltpu.roll(pieces[k], turn, 1) if k <= blocks else pieces[k]
            moved_ref[p, k - 1, rows, :] = jnp.where(lane < turn, before, here)
            before = here

    moves = []
    up, down = at_ref[0], at_ref[1]
    for p in range(planes):
        v = step * planes + p
        dy, dx = offsets_ref[0, v], offsets_ref[1, v]
        turn = dx & (LANES - 1)
        q = jnp.where(dx >= 0, 0, 1)
        moves.append((dy, q))
        g, w = v // share, v % share
        shift = (dx - (w + 1 - q) * MAXV) & (LANES - 1)
        beyond = pltpu.roll(side_ref[q, g], shift, 1)
        here = [pooled_ref[v, :, cut].astype(f32) for cut in cuts]
        store(p, slice(MAXV, MAXV + height), turn, [beyond] + here + [beyond])
        below = jnp.where(dy >= 0, 0, 1)
        source = pl.ds(jnp.where(dy >= 0, up + dy, down + MAXV), MAXV)
        halo = [halo_ref[below ^ (1 - odd), k, source, :] for k in range(blocks + 2)]
        halo[0] = pltpu.roll(halo[0], turn, 1)
        halo[-1] = pltpu.roll(halo[-1], turn, 1)
        store(p, pl.ds(pl.multiple_of(below * (MAXV + height), MAXV), MAXV), turn, halo)
        up = up + jnp.maximum(dy, 0)
        down = down + jnp.maximum(-dy, 0)
    at_ref[0] = up
    at_ref[1] = down

    for p in range(planes):
        dy, q = moves[p]
        for k in range(blocks):
            shifted = moved_ref[p, k + q, pl.ds(MAXV - dy, height), :]
            out_ref[p, :, cuts[k]] = (filtered_ref[k] + FORGET * shifted).astype(bf16)


def merge(pooled, tile, seams, nears, sides, fars, offsets, taps_col):
    planes, height, width = pooled.shape
    blocks = width // LANES
    groups = planes * MAXV // LANES
    vmem, anywhere = pl.BlockSpec(memory_space=pltpu.VMEM), pl.BlockSpec(memory_space=pl.ANY)
    return pl.pallas_call(
        merge_kernel,
        grid=(planes // SLAB,),
        out_shape=jax.ShapeDtypeStruct((planes, height, width), bf16),
        in_specs=[smem(), smem()] + [vmem] * 8 + [anywhere] * 4,
        out_specs=pl.BlockSpec((SLAB, height, width), lambda i: (i, 0, 0)),
        scratch_shapes=[
            pltpu.VMEM((2, blocks + 2, ALL_ROWS + 2 * MAXV, LANES), f32),
            pltpu.VMEM((2, groups, height, LANES), f32),
            pltpu.VMEM((blocks, height + 2 * MAXV, LANES), f32),
            pltpu.VMEM((blocks, height, LANES), f32),
            pltpu.VMEM((SLAB, blocks + 1, height + 2 * MAXV, LANES), f32),
            pltpu.SMEM((2,), jnp.int32),
            pltpu.VMEM(fars[0].shape, bf16),
            pltpu.VMEM(fars[2].shape, bf16),
            pltpu.SemaphoreType.DMA,
        ],
        compiler_params=params(40 * 2**20),
        name="merge",
    )(offsets, taps_col, pooled, tile, *seams, *nears, *sides, *fars)


def pass_on(value, axis):
    count = lax.axis_size(axis)
    return lax.ppermute(value, axis, [(i, i + 1) for i in range(count - 1)])


def pass_back(value, axis):
    count = lax.axis_size(axis)
    return lax.ppermute(value, axis, [(i + 1, i) for i in range(count - 1)])


def trade(value, axis, first):
    pairs = []
    for i in range(first, lax.axis_size(axis) - 1, 2):
        pairs += [(i, i + 1), (i + 1, i)]
    return lax.ppermute(value, axis, pairs)


def far_exchange(state):
    count, far_a, far_b, _, _ = state
    far_b = trade(far_b, "rows", 1)
    far_a = trade(far_a, "rows", 0)
    width = far_a.shape[1]
    last = jnp.concatenate([far_a[:, width - LANES :], far_b[:, width - LANES :]], axis=0)
    first = jnp.concatenate([far_a[:, :LANES], far_b[:, :LANES]], axis=0)
    return count - 1, far_a, far_b, pass_on(last, "cols"), pass_back(first, "cols")


def on_device(frame, taps_row, taps_col, merit, offsets):
    _, height, width = merit.shape
    turned = offsets.T
    near_a, near_b, *fars, more = pool_outer(merit, turned)
    b = trade(near_b, "rows", 1)
    a = trade(near_a, "rows", 0)
    pieces = filter_rows(frame, taps_row, frame.shape[1] // width, a)
    tile = lax.all_to_all(pieces, "cols", split_axis=0, concat_axis=0, tiled=True).reshape(height, width)
    _, *fars = lax.while_loop(lambda state: state[0] > 0, far_exchange, (more.reshape(()), *fars))
    right, left = pool_sides(merit, pieces, fars[2])
    last, first = join(right, left, a, b)
    west, east = pass_on(last, "cols"), pass_back(first, "cols")
    top, bottom = tile[:MAXV], tile[height - MAXV :]
    odd = lax.axis_index("rows") % 2 == 1
    for_b, for_a = jnp.where(odd, bottom, top), jnp.where(odd, top, bottom)
    seam_b = trade(for_b, "rows", 1)
    seam_a = trade(for_a, "rows", 0)
    pooled = pool_all(merit, (for_a, for_b, fars[2], fars[3]))
    return merge(pooled, tile, (seam_a, seam_b), (a, b), (west, east), fars, turned, taps_col)


def solution(mesh):
    in_specs = (P(("rows", "cols"), None), P(), P(), P(None, "rows", "cols"), P())
    out_specs = P(None, "rows", "cols")
    return jax.shard_map(on_device, mesh=mesh, in_specs=in_specs, out_specs=out_specs, check_vma=False)
```

```python
import functools

import jax
import jax.numpy as jnp
from jax import lax
from jax.experimental import pallas as pl
from jax.experimental.pallas import tpu as pltpu
from jax.sharding import PartitionSpec as P

VGRID = 8
MAXV = 8
VELS = VGRID * VGRID
LANES = 128
FORGET = 0.875
SOME_ROWS = 208
ALL_ROWS = VELS * MAXV
SLAB = 16
CHUNK = 16
LIMIT = 58 * 2**20

f32 = jnp.float32
bf16 = jnp.bfloat16


def params(limit=LIMIT):
    return pltpu.CompilerParams(vmem_limit_bytes=limit)


def brief():
    return pl.CostEstimate(flops=1000, bytes_accessed=1000, transcendentals=0)


def smem():
    return pl.BlockSpec(memory_space=pltpu.SMEM)


def filter_rows_kernel(taps_ref, strip_ref, after_ref, out_ref, pad_ref):
    del after_ref
    half = taps_ref.shape[0] // 2
    height, width = strip_ref.shape
    pad_ref[:, :LANES] = jnp.zeros((height, LANES), f32)
    pad_ref[:, LANES + width :] = jnp.zeros((height, LANES), f32)
    pad_ref[:, LANES : LANES + width] = strip_ref[...]
    count, _, span = out_ref.shape
    for piece in range(count):
        start = LANES + piece * span
        total = jnp.zeros((height, span), f32)
        for j in range(taps_ref.shape[0]):
            total = total + taps_ref[j] * pad_ref[:, start + j - half : start + j - half + span]
        out_ref[piece] = total


def filter_rows(strip, taps_row, pieces, after):
    height, width = strip.shape
    return pl.pallas_call(
        filter_rows_kernel,
        out_shape=jax.ShapeDtypeStruct((pieces, height, width // pieces), f32),
        in_specs=[smem(), pl.BlockSpec(memory_space=pltpu.VMEM), pl.BlockSpec(memory_space=pl.ANY)],
        out_specs=pl.BlockSpec(memory_space=pltpu.VMEM),
        scratch_shapes=[pltpu.VMEM((height, width + 2 * LANES), f32)],
        cost_estimate=brief(),
        compiler_params=params(16 * 2**20),
        name="filter_rows",
    )(taps_row, strip, after)


def max_of_three(values):
    total = len(values)
    pairs = [jnp.maximum(values[i], values[i + 1]) for i in range(total - 1)]
    middle = [jnp.maximum(pairs[i - 1], values[i + 1]) for i in range(1, total - 1)]
    return [pairs[0]] + middle + [pairs[-1]]


def pool_chunk(merit_ref, pooled_ref, rows, cols):
    def line(a):
        return max_of_three([merit_ref[a * VGRID + b, rows, cols] for b in range(VGRID)])

    def emit(a, planes):
        for b in range(VGRID):
            pooled_ref[a * VGRID + b, rows, cols] = planes[b]

    last, here = line(0), line(1)
    pair = [jnp.maximum(x, y) for x, y in zip(last, here)]
    emit(0, pair)
    for a in range(2, VGRID):
        after = line(a)
        emit(a - 1, [jnp.maximum(x, y) for x, y in zip(pair, after)])
        pair = [jnp.maximum(x, y) for x, y in zip(here, after)]
        here = after
    emit(VGRID - 1, pair)


def pack_side(pooled_ref, cols, turn, target_ref):
    height = pooled_ref.shape[1]
    lane_group = lax.broadcasted_iota(jnp.int32, (height, LANES), 1) // MAXV
    share = LANES // MAXV
    for g in range(VELS // share):
        total = jnp.zeros((height, LANES), f32)
        for w in range(share):
            edge = pooled_ref[g * share + w, :, cols].astype(f32)
            total = jnp.where(lane_group == w, pltpu.roll(edge, (w + turn) * MAXV % LANES, 1), total)
        target_ref[g] = total.astype(bf16)


def pool_as_they_come(copies, sizes, held_ref, pooled_ref, then=None):
    for copy in copies:
        copy.start()
    for copy, (height, top, width, left) in zip(copies, sizes):
        copy.wait()
        across = width // LANES

        def one(i, carry):
            rows = pl.ds(pl.multiple_of(top + i // across * CHUNK, CHUNK), CHUNK)
            cols = pl.ds(pl.multiple_of(left + i % across * LANES, LANES), LANES)
            pool_chunk(held_ref, pooled_ref, rows, cols)
            return carry

        lax.fori_loop(0, height // CHUNK * across, one, 0)
        if then is not None:
            then(top, left)


def pool_all_kernel(merit_ref, *refs):
    pooled_ref, held_ref, sems = refs[-3:]
    _, height, width = merit_ref.shape
    part = width // 2
    sizes = [(CHUNK, top, part, left) for top in range(0, height, CHUNK) for left in (0, part)]
    copies = []
    for n, (_, top, _, left) in enumerate(sizes):
        at = (slice(None), pl.ds(top, CHUNK), pl.ds(left, part))
        copies.append(pltpu.make_async_copy(merit_ref.at[at], held_ref.at[at], sems.at[n]))
    pool_as_they_come(copies, sizes, held_ref, pooled_ref)


def pool_sides_kernel(merit_ref, after_ref, far_ref, right_ref, left_ref, held_ref, pooled_ref, sems):
    del after_ref, far_ref
    _, height, width = merit_ref.shape
    sizes = [(height, 0, LANES, left) for left in (0, LANES)]
    copies = []
    for n, first in enumerate((0, width - LANES)):
        source = merit_ref.at[:, :, pl.ds(first, LANES)]
        copies.append(pltpu.make_async_copy(source, held_ref.at[:, :, pl.ds(n * LANES, LANES)], sems.at[n]))
    pool_as_they_come(copies, sizes, held_ref, pooled_ref)
    pack_side(pooled_ref, slice(0, LANES), 0, left_ref)
    pack_side(pooled_ref, slice(LANES, 2 * LANES), 1, right_ref)


def pool_outer_kernel(
    offsets_ref, merit_ref, near_a_ref, near_b_ref, far_a_ref, far_b_ref, far_west_ref, far_east_ref, more_ref,
    held_ref, pooled_ref, packed_ref, stage_ref, sems, far_sems,
):
    del far_west_ref, far_east_ref
    _, height, width = merit_ref.shape
    blocks = width // LANES
    odd = lax.axis_index("rows") % 2

    def count(v, sign):
        return jnp.maximum(sign * offsets_ref[0, v], 0)

    up, down = 0, 0
    for v in range(VELS):
        up = up + count(v, 1)
        down = down + count(v, -1)

    part = width // 2
    sizes = [(CHUNK, top, part, left) for top in (0, CHUNK) for left in (0, part)]
    copies = []
    for n, (_, top, _, left) in enumerate(sizes):
        rows, cols = pl.ds(top and height - CHUNK, CHUNK), pl.ds(left, part)
        target = held_ref.at[:, pl.ds(top, CHUNK), cols]
        copies.append(pltpu.make_async_copy(merit_ref.at[:, rows, cols], target, sems.at[n]))

    def pack(top, left):
        edge = top // CHUNK
        mine = range(left // LANES, (left + part) // LANES)

        def tile(v, k):
            return pooled_ref[v, edge * CHUNK : (edge + 1) * CHUNK, k * LANES : (k + 1) * LANES].astype(f32)

        if edge == 0:
            at = 0
            for v in range(VELS):
                for k in mine:
                    packed_ref[0, k, pl.ds(at + MAXV, MAXV), :] = tile(v, k)[:MAXV]
                at = at + count(v, -1)
        else:
            at = up
            for v in range(VELS - 1, -1, -1):
                for k in mine:
                    packed_ref[1, k, pl.ds(at, MAXV), :] = tile(v, k)[CHUNK - MAXV :]
                at = at - count(v, 1)

    pool_as_they_come(copies, sizes, held_ref, pooled_ref, pack)

    for slot, ref in enumerate((near_a_ref, near_b_ref)):
        mine = odd if slot == 1 else 1 - odd
        for k in range(blocks):
            piece = packed_ref[mine, k, MAXV : MAXV + SOME_ROWS, :]
            ref[:, k * LANES : (k + 1) * LANES] = piece.astype(bf16)

    more = jnp.maximum(up, down) > SOME_ROWS
    more_ref[0] = more.astype(jnp.int32)

    @pl.when(more)
    def _():
        for slot, ref in enumerate((far_a_ref, far_b_ref)):
            mine = odd if slot == 1 else 1 - odd
            for k in range(blocks):
                piece = packed_ref[mine, k, MAXV + SOME_ROWS : MAXV + ALL_ROWS, :]
                stage_ref[:, k * LANES : (k + 1) * LANES] = piece.astype(bf16)
            copy = pltpu.make_async_copy(stage_ref, ref, far_sems.at[slot])
            copy.start()
            copy.wait()


def pool_cost(merit):
    return pl.CostEstimate(flops=2 * merit.size, bytes_accessed=merit.size, transcendentals=0)


def pool_all(merit, after):
    anywhere = pl.BlockSpec(memory_space=pl.ANY)
    return pl.pallas_call(
        pool_all_kernel,
        out_shape=pltpu.VMEM(merit.shape, bf16),
        in_specs=[anywhere] * (1 + len(after)),
        out_specs=pl.BlockSpec(memory_space=pltpu.VMEM),
        scratch_shapes=[pltpu.VMEM(merit.shape, bf16), pltpu.SemaphoreType.DMA((2 * merit.shape[1] // CHUNK,))],
        cost_estimate=pool_cost(merit),
        compiler_params=params(48 * 2**20),
        name="pool_all",
    )(merit, *after)


def pool_sides(merit, after, far):
    planes, height, _ = merit.shape
    side = (planes * MAXV // LANES, height, LANES)
    anywhere = pl.BlockSpec(memory_space=pl.ANY)
    return pl.pallas_call(
        pool_sides_kernel,
        out_shape=[pltpu.VMEM(side, bf16)] * 2,
        in_specs=[anywhere] * 3,
        out_specs=[pl.BlockSpec(memory_space=pltpu.VMEM)] * 2,
        scratch_shapes=[pltpu.VMEM((planes, height, 2 * LANES), bf16)] * 2 + [pltpu.SemaphoreType.DMA((2,))],
        cost_estimate=brief(),
        compiler_params=params(),
        name="pool_sides",
    )(merit, after, far)


def pool_outer(merit, offsets):
    planes, height, width = merit.shape
    part = (planes, 2 * CHUNK, width)
    near, far = (SOME_ROWS, width), (ALL_ROWS - SOME_ROWS, width)
    return pl.pallas_call(
        pool_outer_kernel,
        out_shape=[pltpu.VMEM(near, bf16)] * 2
        + [pltpu.HBM(far, bf16)] * 2
        + [pltpu.HBM((2 * far[0], LANES), bf16)] * 2
        + [jax.ShapeDtypeStruct((1,), jnp.int32)],
        in_specs=[smem(), pl.BlockSpec(memory_space=pl.ANY)],
        out_specs=[pl.BlockSpec(memory_space=pltpu.VMEM)] * 2 + [pl.BlockSpec(memory_space=pl.ANY)] * 4 + [smem()],
        scratch_shapes=[
            pltpu.VMEM(part, bf16),
            pltpu.VMEM(part, bf16),
            pltpu.VMEM((2, width // LANES, ALL_ROWS + 2 * MAXV, LANES), f32),
            pltpu.VMEM(far, bf16),
            pltpu.SemaphoreType.DMA((4,)),
            pltpu.SemaphoreType.DMA((2,)),
        ],
        cost_estimate=pool_cost(merit),
        compiler_params=params(),
        name="pool_outer",
    )(offsets, merit)


def join_kernel(right_ref, left_ref, a_ref, b_ref, last_ref, first_ref):
    groups, height, _ = right_ref.shape
    width = a_ref.shape[1]
    for side, out, edge in ((right_ref, last_ref, width - LANES), (left_ref, first_ref, 0)):
        for g in range(groups):
            out[g * height : (g + 1) * height, :] = side[g]
        for e, ref in enumerate((a_ref, b_ref)):
            start = groups * height + e * SOME_ROWS
            out[start : start + SOME_ROWS, :] = ref[:, edge : edge + LANES]


def join(right, left, a, b):
    groups, height, _ = right.shape
    vmem = pl.BlockSpec(memory_space=pltpu.VMEM)
    return pl.pallas_call(
        join_kernel,
        out_shape=[jax.ShapeDtypeStruct((groups * height + 2 * SOME_ROWS, LANES), bf16)] * 2,
        in_specs=[vmem] * 4,
        out_specs=[vmem] * 2,
        cost_estimate=brief(),
        compiler_params=params(16 * 2**20),
        name="join",
    )(right, left, a, b)


def weighted_rows(taps_ref, column_ref, k, count):
    half = taps_ref.shape[0] // 2
    total = jnp.zeros((count, LANES), f32)
    for i in range(taps_ref.shape[0]):
        start = MAXV - half + i
        total = total + taps_ref[i] * column_ref[k, start : start + count, :]
    return total


def merge_kernel(
    offsets_ref, taps_ref, pooled_ref, tile_ref, seam_a_ref, seam_b_ref, near_a_ref, near_b_ref,
    west_ref, east_ref, far_a_ref, far_b_ref, far_west_ref, far_east_ref, out_ref,
    halo_ref, side_ref, column_ref, filtered_ref, moved_ref, at_ref, stage_ref, stage_side_ref, sem,
):
    step = pl.program_id(0)
    planes, height, width = out_ref.shape
    blocks = width // LANES
    groups = VELS * MAXV // LANES
    share = LANES // MAXV
    odd = lax.axis_index("rows") % 2
    cuts = [slice(k * LANES, (k + 1) * LANES) for k in range(blocks)]

    @pl.when(step == 0)
    def _():
        up, down = 0, 0
        for v in range(VELS):
            up = up + jnp.maximum(offsets_ref[0, v], 0)
            down = down + jnp.maximum(-offsets_ref[0, v], 0)
        at_ref[0] = 0
        at_ref[1] = 0
        near = slice(MAXV, MAXV + SOME_ROWS)
        start = groups * height
        for e, ref in enumerate((near_a_ref, near_b_ref)):
            for k in range(blocks):
                halo_ref[e, k + 1, near, :] = ref[:, cuts[k]].astype(f32)
            part = slice(start + e * SOME_ROWS, start + (e + 1) * SOME_ROWS)
            halo_ref[e, 0, near, :] = west_ref[part, :].astype(f32)
            halo_ref[e, blocks + 1, near, :] = east_ref[part, :].astype(f32)
        for e, ref in enumerate((west_ref, east_ref)):
            for g in range(groups):
                side_ref[e, g] = ref[g * height : (g + 1) * height, :].astype(f32)
        for k in range(blocks):
            a, b = seam_a_ref[:, cuts[k]], seam_b_ref[:, cuts[k]]
            column_ref[k, :MAXV, :] = jnp.where(odd == 1, a, b)
            column_ref[k, MAXV : MAXV + height, :] = tile_ref[:, cuts[k]]
            column_ref[k, MAXV + height :, :] = jnp.where(odd == 1, b, a)
        for k in range(blocks):
            filtered_ref[k] = weighted_rows(taps_ref, column_ref, k, height)

        @pl.when(jnp.maximum(up, down) > SOME_ROWS)
        def _():
            def bring(source, target):
                copy = pltpu.make_async_copy(source, target, sem)
                copy.start()
                copy.wait()

            far = slice(MAXV + SOME_ROWS, MAXV + ALL_ROWS)
            count = ALL_ROWS - SOME_ROWS
            for e, ref in enumerate((far_a_ref, far_b_ref)):
                bring(ref, stage_ref)
                for k in range(blocks):
                    halo_ref[e, k + 1, far, :] = stage_ref[:, cuts[k]].astype(f32)
            for k, ref in ((0, far_west_ref), (blocks + 1, far_east_ref)):
                bring(ref, stage_side_ref)
                for e in range(2):
                    halo_ref[e, k, far, :] = stage_side_ref[e * count : (e + 1) * count, :].astype(f32)

    def store(p, rows, turn, pieces):
        lane = lax.broadcasted_iota(jnp.int32, pieces[1].shape, 1)
        before = pieces[0]
        for k in range(1, blocks + 2):
            here = pltpu.roll(pieces[k], turn, 1) if k <= blocks else pieces[k]
            moved_ref[p, k - 1, rows, :] = jnp.where(lane < turn, before, here)
            before = here

    moves = []
    up, down = at_ref[0], at_ref[1]
    for p in range(planes):
        v = step * planes + p
        dy, dx = offsets_ref[0, v], offsets_ref[1, v]
        turn = dx & (LANES - 1)
        q = jnp.where(dx >= 0, 0, 1)
        moves.append((dy, q))
        g, w = v // share, v % share
        shift = (dx - (w + 1 - q) * MAXV) & (LANES - 1)
        beyond = pltpu.roll(side_ref[q, g], shift, 1)
        here = [pooled_ref[v, :, cut].astype(f32) for cut in cuts]
        store(p, slice(MAXV, MAXV + height), turn, [beyond] + here + [beyond])
        below = jnp.where(dy >= 0, 0, 1)
        source = pl.ds(jnp.where(dy >= 0, up + dy, down + MAXV), MAXV)
        halo = [halo_ref[below ^ (1 - odd), k, source, :] for k in range(blocks + 2)]
        halo[0] = pltpu.roll(halo[0], turn, 1)
        halo[-1] = pltpu.roll(halo[-1], turn, 1)
        store(p, pl.ds(pl.multiple_of(below * (MAXV + height), MAXV), MAXV), turn, halo)
        up = up + jnp.maximum(dy, 0)
        down = down + jnp.maximum(-dy, 0)
    at_ref[0] = up
    at_ref[1] = down

    for p in range(planes):
        dy, q = moves[p]
        for k in range(blocks):
            shifted = moved_ref[p, k + q, pl.ds(MAXV - dy, height), :]
            out_ref[p, :, cuts[k]] = (filtered_ref[k] + FORGET * shifted).astype(bf16)


def merge(pooled, tile, seams, nears, sides, fars, offsets, taps_col):
    planes, height, width = pooled.shape
    blocks = width // LANES
    groups = planes * MAXV // LANES
    vmem, anywhere = pl.BlockSpec(memory_space=pltpu.VMEM), pl.BlockSpec(memory_space=pl.ANY)
    return pl.pallas_call(
        merge_kernel,
        grid=(planes // SLAB,),
        out_shape=jax.ShapeDtypeStruct((planes, height, width), bf16),
        in_specs=[smem(), smem()] + [vmem] * 8 + [anywhere] * 4,
        out_specs=pl.BlockSpec((SLAB, height, width), lambda i: (i, 0, 0)),
        scratch_shapes=[
            pltpu.VMEM((2, blocks + 2, ALL_ROWS + 2 * MAXV, LANES), f32),
            pltpu.VMEM((2, groups, height, LANES), f32),
            pltpu.VMEM((blocks, height + 2 * MAXV, LANES), f32),
            pltpu.VMEM((blocks, height, LANES), f32),
            pltpu.VMEM((SLAB, blocks + 1, height + 2 * MAXV, LANES), f32),
            pltpu.SMEM((2,), jnp.int32),
            pltpu.VMEM(fars[0].shape, bf16),
            pltpu.VMEM(fars[2].shape, bf16),
            pltpu.SemaphoreType.DMA,
        ],
        compiler_params=params(40 * 2**20),
        name="merge",
    )(offsets, taps_col, pooled, tile, *seams, *nears, *sides, *fars)


def pass_on(value, axis):
    count = lax.axis_size(axis)
    return lax.ppermute(value, axis, [(i, i + 1) for i in range(count - 1)])


def pass_back(value, axis):
    count = lax.axis_size(axis)
    return lax.ppermute(value, axis, [(i + 1, i) for i in range(count - 1)])


def trade(value, axis, first):
    pairs = []
    for i in range(first, lax.axis_size(axis) - 1, 2):
        pairs += [(i, i + 1), (i + 1, i)]
    return lax.ppermute(value, axis, pairs)


def far_exchange(state):
    count, far_a, far_b, _, _ = state
    far_b = trade(far_b, "rows", 1)
    far_a = trade(far_a, "rows", 0)
    width = far_a.shape[1]
    last = jnp.concatenate([far_a[:, width - LANES :], far_b[:, width - LANES :]], axis=0)
    first = jnp.concatenate([far_a[:, :LANES], far_b[:, :LANES]], axis=0)
    return count - 1, far_a, far_b, pass_on(last, "cols"), pass_back(first, "cols")


def on_device(frame, taps_row, taps_col, merit, offsets):
    _, height, width = merit.shape
    turned = offsets.T
    near_a, near_b, *fars, more = pool_outer(merit, turned)
    b = trade(near_b, "rows", 1)
    a = trade(near_a, "rows", 0)
    pieces = filter_rows(frame, taps_row, frame.shape[1] // width, a)
    tile = lax.all_to_all(pieces, "cols", split_axis=0, concat_axis=0, tiled=True).reshape(height, width)
    _, *fars = lax.while_loop(lambda state: state[0] > 0, far_exchange, (more.reshape(()), *fars))
    right, left = pool_sides(merit, pieces, fars[2])
    last, first = join(right, left, a, b)
    west, east = pass_on(last, "cols"), pass_back(first, "cols")
    top, bottom = tile[:MAXV], tile[height - MAXV :]
    odd = lax.axis_index("rows") % 2 == 1
    for_b, for_a = jnp.where(odd, bottom, top), jnp.where(odd, top, bottom)
    seam_b = trade(for_b, "rows", 1)
    seam_a = trade(for_a, "rows", 0)
    pooled = pool_all(merit, (for_a, for_b, fars[2], fars[3]))
    return merge(pooled, tile, (seam_a, seam_b), (a, b), (west, east), fars, turned, taps_col)


def solution(mesh):
    in_specs = (P(("rows", "cols"), None), P(), P(), P(None, "rows", "cols"), P())
    out_specs = P(None, "rows", "cols")
    return jax.shard_map(on_device, mesh=mesh, in_specs=in_specs, out_specs=out_specs, check_vma=False)
```

```python
import functools

import jax
import jax.numpy as jnp
from jax import lax
from jax.experimental import pallas as pl
from jax.experimental.pallas import tpu as pltpu
from jax.sharding import PartitionSpec as P

VGRID = 8
MAXV = 8
VELS = VGRID * VGRID
LANES = 128
FORGET = 0.875
SOME_ROWS = 208
ALL_ROWS = VELS * MAXV
SLAB = 16
CHUNK = 16
LIMIT = 58 * 2**20

f32 = jnp.float32
bf16 = jnp.bfloat16


def params(limit=LIMIT):
    return pltpu.CompilerParams(vmem_limit_bytes=limit)


def brief():
    return pl.CostEstimate(flops=1000, bytes_accessed=1000, transcendentals=0)


def smem():
    return pl.BlockSpec(memory_space=pltpu.SMEM)


def filter_rows_kernel(taps_ref, strip_ref, after_ref, out_ref, pad_ref, done_ref, sems):
    del after_ref
    half = taps_ref.shape[0] // 2
    height, width = strip_ref.shape
    pad_ref[:, :LANES] = jnp.zeros((height, LANES), f32)
    pad_ref[:, LANES + width :] = jnp.zeros((height, LANES), f32)
    pad_ref[:, LANES : LANES + width] = strip_ref[...]
    count, _, span = out_ref.shape
    copies = []
    for piece in range(count):
        start = LANES + piece * span
        total = jnp.zeros((height, span), f32)
        for j in range(taps_ref.shape[0]):
            total = total + taps_ref[j] * pad_ref[:, start + j - half : start + j - half + span]
        done_ref[piece] = total
        copies.append(pltpu.make_async_copy(done_ref.at[piece], out_ref.at[piece], sems.at[piece]))
        copies[-1].start()
    for copy in copies:
        copy.wait()


def filter_rows(strip, taps_row, pieces, after):
    height, width = strip.shape
    return pl.pallas_call(
        filter_rows_kernel,
        out_shape=jax.ShapeDtypeStruct((pieces, height, width // pieces), f32),
        in_specs=[smem(), pl.BlockSpec(memory_space=pltpu.VMEM), pl.BlockSpec(memory_space=pl.ANY)],
        out_specs=pl.BlockSpec(memory_space=pl.ANY),
        scratch_shapes=[
            pltpu.VMEM((height, width + 2 * LANES), f32),
            pltpu.VMEM((pieces, height, width // pieces), f32),
            pltpu.SemaphoreType.DMA((pieces,)),
        ],
        cost_estimate=brief(),
        compiler_params=params(16 * 2**20),
        name="filter_rows",
    )(taps_row, strip, after)


def max_of_three(values):
    total = len(values)
    pairs = [jnp.maximum(values[i], values[i + 1]) for i in range(total - 1)]
    middle = [jnp.maximum(pairs[i - 1], values[i + 1]) for i in range(1, total - 1)]
    return [pairs[0]] + middle + [pairs[-1]]


def pool_chunk(merit_ref, pooled_ref, rows, cols):
    def line(a):
        return max_of_three([merit_ref[a * VGRID + b, rows, cols] for b in range(VGRID)])

    def emit(a, planes):
        for b in range(VGRID):
            pooled_ref[a * VGRID + b, rows, cols] = planes[b]

    last, here = line(0), line(1)
    pair = [jnp.maximum(x, y) for x, y in zip(last, here)]
    emit(0, pair)
    for a in range(2, VGRID):
        after = line(a)
        emit(a - 1, [jnp.maximum(x, y) for x, y in zip(pair, after)])
        pair = [jnp.maximum(x, y) for x, y in zip(here, after)]
        here = after
    emit(VGRID - 1, pair)


def pack_side(pooled_ref, cols, turn, target_ref):
    height = pooled_ref.shape[1]
    lane_group = lax.broadcasted_iota(jnp.int32, (height, LANES), 1) // MAXV
    share = LANES // MAXV
    for g in range(VELS // share):
        total = jnp.zeros((height, LANES), f32)
        for w in range(share):
            edge = pooled_ref[g * share + w, :, cols].astype(f32)
            total = jnp.where(lane_group == w, pltpu.roll(edge, (w + turn) * MAXV % LANES, 1), total)
        target_ref[g] = total.astype(bf16)


def pool_as_they_come(copies, sizes, held_ref, pooled_ref, then=None):
    for copy in copies:
        copy.start()
    for copy, (height, top, width, left) in zip(copies, sizes):
        copy.wait()
        across = width // LANES

        def one(i, carry):
            rows = pl.ds(pl.multiple_of(top + i // across * CHUNK, CHUNK), CHUNK)
            cols = pl.ds(pl.multiple_of(left + i % across * LANES, LANES), LANES)
            pool_chunk(held_ref, pooled_ref, rows, cols)
            return carry

        lax.fori_loop(0, height // CHUNK * across, one, 0)
        if then is not None:
            then(top, left)


def pool_all_kernel(merit_ref, *refs):
    pooled_ref, held_ref, sems = refs[-3:]
    _, height, width = merit_ref.shape
    part = width // 2
    sizes = [(CHUNK, top, part, left) for top in range(0, height, CHUNK) for left in (0, part)]
    copies = []
    for n, (_, top, _, left) in enumerate(sizes):
        at = (slice(None), pl.ds(top, CHUNK), pl.ds(left, part))
        copies.append(pltpu.make_async_copy(merit_ref.at[at], held_ref.at[at], sems.at[n]))
    pool_as_they_come(copies, sizes, held_ref, pooled_ref)


def pool_sides_kernel(merit_ref, after_ref, far_ref, right_ref, left_ref, held_ref, pooled_ref, sems):
    del after_ref, far_ref
    _, height, width = merit_ref.shape
    sizes = [(height, 0, LANES, left) for left in (0, LANES)]
    copies = []
    for n, first in enumerate((0, width - LANES)):
        source = merit_ref.at[:, :, pl.ds(first, LANES)]
        copies.append(pltpu.make_async_copy(source, held_ref.at[:, :, pl.ds(n * LANES, LANES)], sems.at[n]))
    pool_as_they_come(copies, sizes, held_ref, pooled_ref)
    pack_side(pooled_ref, slice(0, LANES), 0, left_ref)
    pack_side(pooled_ref, slice(LANES, 2 * LANES), 1, right_ref)


def pool_outer_kernel(
    offsets_ref, merit_ref, near_a_ref, near_b_ref, far_a_ref, far_b_ref, far_west_ref, far_east_ref, more_ref,
    held_ref, pooled_ref, packed_ref, stage_ref, sems, far_sems,
):
    del far_west_ref, far_east_ref
    _, height, width = merit_ref.shape
    blocks = width // LANES
    odd = lax.axis_index("rows") % 2

    def count(v, sign):
        return jnp.maximum(sign * offsets_ref[0, v], 0)

    up, down = 0, 0
    for v in range(VELS):
        up = up + count(v, 1)
        down = down + count(v, -1)

    part = width // 2
    sizes = [(CHUNK, top, part, left) for top in (0, CHUNK) for left in (0, part)]
    copies = []
    for n, (_, top, _, left) in enumerate(sizes):
        rows, cols = pl.ds(top and height - CHUNK, CHUNK), pl.ds(left, part)
        target = held_ref.at[:, pl.ds(top, CHUNK), cols]
        copies.append(pltpu.make_async_copy(merit_ref.at[:, rows, cols], target, sems.at[n]))

    def pack(top, left):
        edge = top // CHUNK
        mine = range(left // LANES, (left + part) // LANES)

        def tile(v, k):
            return pooled_ref[v, edge * CHUNK : (edge + 1) * CHUNK, k * LANES : (k + 1) * LANES].astype(f32)

        if edge == 0:
            at = 0
            for v in range(VELS):
                for k in mine:
                    packed_ref[0, k, pl.ds(at + MAXV, MAXV), :] = tile(v, k)[:MAXV]
                at = at + count(v, -1)
        else:
            at = up
            for v in range(VELS - 1, -1, -1):
                for k in mine:
                    packed_ref[1, k, pl.ds(at, MAXV), :] = tile(v, k)[CHUNK - MAXV :]
                at = at - count(v, 1)

    pool_as_they_come(copies, sizes, held_ref, pooled_ref, pack)

    for slot, ref in enumerate((near_a_ref, near_b_ref)):
        mine = odd if slot == 1 else 1 - odd
        for k in range(blocks):
            piece = packed_ref[mine, k, MAXV : MAXV + SOME_ROWS, :]
            ref[:, k * LANES : (k + 1) * LANES] = piece.astype(bf16)

    more = jnp.maximum(up, down) > SOME_ROWS
    more_ref[0] = more.astype(jnp.int32)

    @pl.when(more)
    def _():
        for slot, ref in enumerate((far_a_ref, far_b_ref)):
            mine = odd if slot == 1 else 1 - odd
            for k in range(blocks):
                piece = packed_ref[mine, k, MAXV + SOME_ROWS : MAXV + ALL_ROWS, :]
                stage_ref[:, k * LANES : (k + 1) * LANES] = piece.astype(bf16)
            copy = pltpu.make_async_copy(stage_ref, ref, far_sems.at[slot])
            copy.start()
            copy.wait()


def pool_cost(merit):
    return pl.CostEstimate(flops=2 * merit.size, bytes_accessed=merit.size, transcendentals=0)


def pool_all(merit, after):
    anywhere = pl.BlockSpec(memory_space=pl.ANY)
    return pl.pallas_call(
        pool_all_kernel,
        out_shape=pltpu.VMEM(merit.shape, bf16),
        in_specs=[anywhere] * (1 + len(after)),
        out_specs=pl.BlockSpec(memory_space=pltpu.VMEM),
        scratch_shapes=[pltpu.VMEM(merit.shape, bf16), pltpu.SemaphoreType.DMA((2 * merit.shape[1] // CHUNK,))],
        cost_estimate=pool_cost(merit),
        compiler_params=params(48 * 2**20),
        name="pool_all",
    )(merit, *after)


def pool_sides(merit, after, far):
    planes, height, _ = merit.shape
    side = (planes * MAXV // LANES, height, LANES)
    anywhere = pl.BlockSpec(memory_space=pl.ANY)
    return pl.pallas_call(
        pool_sides_kernel,
        out_shape=[pltpu.VMEM(side, bf16)] * 2,
        in_specs=[anywhere] * 3,
        out_specs=[pl.BlockSpec(memory_space=pltpu.VMEM)] * 2,
        scratch_shapes=[pltpu.VMEM((planes, height, 2 * LANES), bf16)] * 2 + [pltpu.SemaphoreType.DMA((2,))],
        cost_estimate=brief(),
        compiler_params=params(),
        name="pool_sides",
    )(merit, after, far)


def pool_outer(merit, offsets):
    planes, height, width = merit.shape
    part = (planes, 2 * CHUNK, width)
    near, far = (SOME_ROWS, width), (ALL_ROWS - SOME_ROWS, width)
    return pl.pallas_call(
        pool_outer_kernel,
        out_shape=[pltpu.VMEM(near, bf16)] * 2
        + [pltpu.HBM(far, bf16)] * 2
        + [pltpu.HBM((2 * far[0], LANES), bf16)] * 2
        + [jax.ShapeDtypeStruct((1,), jnp.int32)],
        in_specs=[smem(), pl.BlockSpec(memory_space=pl.ANY)],
        out_specs=[pl.BlockSpec(memory_space=pltpu.VMEM)] * 2 + [pl.BlockSpec(memory_space=pl.ANY)] * 4 + [smem()],
        scratch_shapes=[
            pltpu.VMEM(part, bf16),
            pltpu.VMEM(part, bf16),
            pltpu.VMEM((2, width // LANES, ALL_ROWS + 2 * MAXV, LANES), f32),
            pltpu.VMEM(far, bf16),
            pltpu.SemaphoreType.DMA((4,)),
            pltpu.SemaphoreType.DMA((2,)),
        ],
        cost_estimate=pool_cost(merit),
        compiler_params=params(),
        name="pool_outer",
    )(offsets, merit)


def join_kernel(right_ref, left_ref, a_ref, b_ref, last_ref, first_ref):
    groups, height, _ = right_ref.shape
    width = a_ref.shape[1]
    for side, out, edge in ((right_ref, last_ref, width - LANES), (left_ref, first_ref, 0)):
        for g in range(groups):
            out[g * height : (g + 1) * height, :] = side[g]
        for e, ref in enumerate((a_ref, b_ref)):
            start = groups * height + e * SOME_ROWS
            out[start : start + SOME_ROWS, :] = ref[:, edge : edge + LANES]


def join(right, left, a, b):
    groups, height, _ = right.shape
    vmem = pl.BlockSpec(memory_space=pltpu.VMEM)
    return pl.pallas_call(
        join_kernel,
        out_shape=[jax.ShapeDtypeStruct((groups * height + 2 * SOME_ROWS, LANES), bf16)] * 2,
        in_specs=[vmem] * 4,
        out_specs=[vmem] * 2,
        cost_estimate=brief(),
        compiler_params=params(16 * 2**20),
        name="join",
    )(right, left, a, b)


def weighted_rows(taps_ref, column_ref, k, count):
    half = taps_ref.shape[0] // 2
    total = jnp.zeros((count, LANES), f32)
    for i in range(taps_ref.shape[0]):
        start = MAXV - half + i
        total = total + taps_ref[i] * column_ref[k, start : start + count, :]
    return total


def merge_kernel(
    offsets_ref, taps_ref, pooled_ref, tile_ref, seam_a_ref, seam_b_ref, near_a_ref, near_b_ref,
    west_ref, east_ref, far_a_ref, far_b_ref, far_west_ref, far_east_ref, out_ref,
    halo_ref, side_ref, column_ref, filtered_ref, moved_ref, at_ref, stage_ref, stage_side_ref, sem,
):
    step = pl.program_id(0)
    planes, height, width = out_ref.shape
    blocks = width // LANES
    groups = VELS * MAXV // LANES
    share = LANES // MAXV
    odd = lax.axis_index("rows") % 2
    cuts = [slice(k * LANES, (k + 1) * LANES) for k in range(blocks)]

    @pl.when(step == 0)
    def _():
        up, down = 0, 0
        for v in range(VELS):
            up = up + jnp.maximum(offsets_ref[0, v], 0)
            down = down + jnp.maximum(-offsets_ref[0, v], 0)
        at_ref[0] = 0
        at_ref[1] = 0
        near = slice(MAXV, MAXV + SOME_ROWS)
        start = groups * height
        for e, ref in enumerate((near_a_ref, near_b_ref)):
            for k in range(blocks):
                halo_ref[e, k + 1, near, :] = ref[:, cuts[k]].astype(f32)
            part = slice(start + e * SOME_ROWS, start + (e + 1) * SOME_ROWS)
            halo_ref[e, 0, near, :] = west_ref[part, :].astype(f32)
            halo_ref[e, blocks + 1, near, :] = east_ref[part, :].astype(f32)
        for e, ref in enumerate((west_ref, east_ref)):
            for g in range(groups):
                side_ref[e, g] = ref[g * height : (g + 1) * height, :].astype(f32)
        for k in range(blocks):
            a, b = seam_a_ref[:, cuts[k]], seam_b_ref[:, cuts[k]]
            column_ref[k, :MAXV, :] = jnp.where(odd == 1, a, b)
            column_ref[k, MAXV : MAXV + height, :] = tile_ref[:, cuts[k]]
            column_ref[k, MAXV + height :, :] = jnp.where(odd == 1, b, a)
        for k in range(blocks):
            filtered_ref[k] = weighted_rows(taps_ref, column_ref, k, height)

        @pl.when(jnp.maximum(up, down) > SOME_ROWS)
        def _():
            def bring(source, target):
                copy = pltpu.make_async_copy(source, target, sem)
                copy.start()
                copy.wait()

            far = slice(MAXV + SOME_ROWS, MAXV + ALL_ROWS)
            count = ALL_ROWS - SOME_ROWS
            for e, ref in enumerate((far_a_ref, far_b_ref)):
                bring(ref, stage_ref)
                for k in range(blocks):
                    halo_ref[e, k + 1, far, :] = stage_ref[:, cuts[k]].astype(f32)
            for k, ref in ((0, far_west_ref), (blocks + 1, far_east_ref)):
                bring(ref, stage_side_ref)
                for e in range(2):
                    halo_ref[e, k, far, :] = stage_side_ref[e * count : (e + 1) * count, :].astype(f32)

    def store(p, rows, turn, pieces):
        lane = lax.broadcasted_iota(jnp.int32, pieces[1].shape, 1)
        before = pieces[0]
        for k in range(1, blocks + 2):
            here = pltpu.roll(pieces[k], turn, 1) if k <= blocks else pieces[k]
            moved_ref[p, k - 1, rows, :] = jnp.where(lane < turn, before, here)
            before = here

    moves = []
    up, down = at_ref[0], at_ref[1]
    for p in range(planes):
        v = step * planes + p
        dy, dx = offsets_ref[0, v], offsets_ref[1, v]
        turn = dx & (LANES - 1)
        q = jnp.where(dx >= 0, 0, 1)
        moves.append((dy, q))
        g, w = v // share, v % share
        shift = (dx - (w + 1 - q) * MAXV) & (LANES - 1)
        beyond = pltpu.roll(side_ref[q, g], shift, 1)
        here = [pooled_ref[v, :, cut].astype(f32) for cut in cuts]
        store(p, slice(MAXV, MAXV + height), turn, [beyond] + here + [beyond])
        below = jnp.where(dy >= 0, 0, 1)
        source = pl.ds(jnp.where(dy >= 0, up + dy, down + MAXV), MAXV)
        halo = [halo_ref[below ^ (1 - odd), k, source, :] for k in range(blocks + 2)]
        halo[0] = pltpu.roll(halo[0], turn, 1)
        halo[-1] = pltpu.roll(halo[-1], turn, 1)
        store(p, pl.ds(pl.multiple_of(below * (MAXV + height), MAXV), MAXV), turn, halo)
        up = up + jnp.maximum(dy, 0)
        down = down + jnp.maximum(-dy, 0)
    at_ref[0] = up
    at_ref[1] = down

    for p in range(planes):
        dy, q = moves[p]
        for k in range(blocks):
            shifted = moved_ref[p, k + q, pl.ds(MAXV - dy, height), :]
            out_ref[p, :, cuts[k]] = (filtered_ref[k] + FORGET * shifted).astype(bf16)


def merge(pooled, tile, seams, nears, sides, fars, offsets, taps_col):
    planes, height, width = pooled.shape
    blocks = width // LANES
    groups = planes * MAXV // LANES
    vmem, anywhere = pl.BlockSpec(memory_space=pltpu.VMEM), pl.BlockSpec(memory_space=pl.ANY)
    return pl.pallas_call(
        merge_kernel,
        grid=(planes // SLAB,),
        out_shape=jax.ShapeDtypeStruct((planes, height, width), bf16),
        in_specs=[smem(), smem()] + [vmem] * 8 + [anywhere] * 4,
        out_specs=pl.BlockSpec((SLAB, height, width), lambda i: (i, 0, 0)),
        scratch_shapes=[
            pltpu.VMEM((2, blocks + 2, ALL_ROWS + 2 * MAXV, LANES), f32),
            pltpu.VMEM((2, groups, height, LANES), f32),
            pltpu.VMEM((blocks, height + 2 * MAXV, LANES), f32),
            pltpu.VMEM((blocks, height, LANES), f32),
            pltpu.VMEM((SLAB, blocks + 1, height + 2 * MAXV, LANES), f32),
            pltpu.SMEM((2,), jnp.int32),
            pltpu.VMEM(fars[0].shape, bf16),
            pltpu.VMEM(fars[2].shape, bf16),
            pltpu.SemaphoreType.DMA,
        ],
        compiler_params=params(40 * 2**20),
        name="merge",
    )(offsets, taps_col, pooled, tile, *seams, *nears, *sides, *fars)


def pass_on(value, axis):
    count = lax.axis_size(axis)
    return lax.ppermute(value, axis, [(i, i + 1) for i in range(count - 1)])


def pass_back(value, axis):
    count = lax.axis_size(axis)
    return lax.ppermute(value, axis, [(i + 1, i) for i in range(count - 1)])


def trade(value, axis, first):
    pairs = []
    for i in range(first, lax.axis_size(axis) - 1, 2):
        pairs += [(i, i + 1), (i + 1, i)]
    return lax.ppermute(value, axis, pairs)


def far_exchange(state):
    count, far_a, far_b, _, _ = state
    far_b = trade(far_b, "rows", 1)
    far_a = trade(far_a, "rows", 0)
    width = far_a.shape[1]
    last = jnp.concatenate([far_a[:, width - LANES :], far_b[:, width - LANES :]], axis=0)
    first = jnp.concatenate([far_a[:, :LANES], far_b[:, :LANES]], axis=0)
    return count - 1, far_a, far_b, pass_on(last, "cols"), pass_back(first, "cols")


def on_device(frame, taps_row, taps_col, merit, offsets):
    _, height, width = merit.shape
    turned = offsets.T
    near_a, near_b, *fars, more = pool_outer(merit, turned)
    b = trade(near_b, "rows", 1)
    a = trade(near_a, "rows", 0)
    pieces = filter_rows(frame, taps_row, frame.shape[1] // width, a)
    tile = lax.all_to_all(pieces, "cols", split_axis=0, concat_axis=0, tiled=True).reshape(height, width)
    _, *fars = lax.while_loop(lambda state: state[0] > 0, far_exchange, (more.reshape(()), *fars))
    fars = [pltpu.with_memory_space_constraint(x, pltpu.HBM) for x in fars]
    right, left = pool_sides(merit, pieces, fars[2])
    last, first = join(right, left, a, b)
    west, east = pass_on(last, "cols"), pass_back(first, "cols")
    top, bottom = tile[:MAXV], tile[height - MAXV :]
    odd = lax.axis_index("rows") % 2 == 1
    for_b, for_a = jnp.where(odd, bottom, top), jnp.where(odd, top, bottom)
    seam_b = trade(for_b, "rows", 1)
    seam_a = trade(for_a, "rows", 0)
    pooled = pool_all(merit, (for_a, for_b, fars[2], fars[3]))
    return merge(pooled, tile, (seam_a, seam_b), (a, b), (west, east), fars, turned, taps_col)


def solution(mesh):
    in_specs = (P(("rows", "cols"), None), P(), P(), P(None, "rows", "cols"), P())
    out_specs = P(None, "rows", "cols")
    return jax.shard_map(on_device, mesh=mesh, in_specs=in_specs, out_specs=out_specs, check_vma=False)
```

```python
import functools

import jax
import jax.numpy as jnp
from jax import lax
from jax.experimental import pallas as pl
from jax.experimental.pallas import tpu as pltpu
from jax.sharding import PartitionSpec as P

VGRID = 8
MAXV = 8
VELS = VGRID * VGRID
LANES = 128
FORGET = 0.875
SOME_ROWS = 208
ALL_ROWS = VELS * MAXV
SLAB = 16
CHUNK = 16
LIMIT = 58 * 2**20

f32 = jnp.float32
bf16 = jnp.bfloat16


def params(limit=LIMIT):
    return pltpu.CompilerParams(vmem_limit_bytes=limit)


def brief():
    return pl.CostEstimate(flops=1000, bytes_accessed=1000, transcendentals=0)


def smem():
    return pl.BlockSpec(memory_space=pltpu.SMEM)


def filter_rows_kernel(taps_ref, strip_ref, after_ref, out_ref, pad_ref):
    del after_ref
    half = taps_ref.shape[0] // 2
    height, width = strip_ref.shape
    pad_ref[:, :LANES] = jnp.zeros((height, LANES), f32)
    pad_ref[:, LANES + width :] = jnp.zeros((height, LANES), f32)
    pad_ref[:, LANES : LANES + width] = strip_ref[...]
    count, _, span = out_ref.shape
    for piece in range(count):
        start = LANES + piece * span
        total = jnp.zeros((height, span), f32)
        for j in range(taps_ref.shape[0]):
            total = total + taps_ref[j] * pad_ref[:, start + j - half : start + j - half + span]
        out_ref[piece] = total


def filter_rows(strip, taps_row, pieces, after):
    height, width = strip.shape
    return pl.pallas_call(
        filter_rows_kernel,
        out_shape=jax.ShapeDtypeStruct((pieces, height, width // pieces), f32),
        in_specs=[smem(), pl.BlockSpec(memory_space=pltpu.VMEM), pl.BlockSpec(memory_space=pl.ANY)],
        out_specs=pl.BlockSpec(memory_space=pltpu.VMEM),
        scratch_shapes=[pltpu.VMEM((height, width + 2 * LANES), f32)],
        cost_estimate=brief(),
        compiler_params=params(16 * 2**20),
        name="filter_rows",
    )(taps_row, strip, after)


def max_of_three(values):
    total = len(values)
    pairs = [jnp.maximum(values[i], values[i + 1]) for i in range(total - 1)]
    middle = [jnp.maximum(pairs[i - 1], values[i + 1]) for i in range(1, total - 1)]
    return [pairs[0]] + middle + [pairs[-1]]


def pool_chunk(merit_ref, pooled_ref, rows, cols):
    def line(a):
        return max_of_three([merit_ref[a * VGRID + b, rows, cols] for b in range(VGRID)])

    def emit(a, planes):
        for b in range(VGRID):
            pooled_ref[a * VGRID + b, rows, cols] = planes[b]

    last, here = line(0), line(1)
    pair = [jnp.maximum(x, y) for x, y in zip(last, here)]
    emit(0, pair)
    for a in range(2, VGRID):
        after = line(a)
        emit(a - 1, [jnp.maximum(x, y) for x, y in zip(pair, after)])
        pair = [jnp.maximum(x, y) for x, y in zip(here, after)]
        here = after
    emit(VGRID - 1, pair)


def pack_side(pooled_ref, cols, turn, target_ref):
    height = pooled_ref.shape[1]
    lane_group = lax.broadcasted_iota(jnp.int32, (height, LANES), 1) // MAXV
    share = LANES // MAXV
    for g in range(VELS // share):
        total = jnp.zeros((height, LANES), f32)
        for w in range(share):
            edge = pooled_ref[g * share + w, :, cols].astype(f32)
            total = jnp.where(lane_group == w, pltpu.roll(edge, (w + turn) * MAXV % LANES, 1), total)
        target_ref[g] = total.astype(bf16)


def pool_as_they_come(copies, sizes, held_ref, pooled_ref, then=None):
    for copy in copies:
        copy.start()
    for copy, (height, top, width, left) in zip(copies, sizes):
        copy.wait()
        across = width // LANES

        def one(i, carry):
            rows = pl.ds(pl.multiple_of(top + i // across * CHUNK, CHUNK), CHUNK)
            cols = pl.ds(pl.multiple_of(left + i % across * LANES, LANES), LANES)
            pool_chunk(held_ref, pooled_ref, rows, cols)
            return carry

        lax.fori_loop(0, height // CHUNK * across, one, 0)
        if then is not None:
            then(top, left)


def pool_all_kernel(merit_ref, *refs):
    pooled_ref, held_ref, sems = refs[-3:]
    _, height, width = merit_ref.shape
    part = width // 2
    sizes = [(CHUNK, top, part, left) for top in range(0, height, CHUNK) for left in (0, part)]
    copies = []
    for n, (_, top, _, left) in enumerate(sizes):
        at = (slice(None), pl.ds(top, CHUNK), pl.ds(left, part))
        copies.append(pltpu.make_async_copy(merit_ref.at[at], held_ref.at[at], sems.at[n]))
    pool_as_they_come(copies, sizes, held_ref, pooled_ref)


def pool_sides_kernel(merit_ref, after_ref, far_ref, right_ref, left_ref, held_ref, pooled_ref, sems):
    del after_ref, far_ref
    _, height, width = merit_ref.shape
    sizes = [(height, 0, LANES, left) for left in (0, LANES)]
    copies = []
    for n, first in enumerate((0, width - LANES)):
        source = merit_ref.at[:, :, pl.ds(first, LANES)]
        copies.append(pltpu.make_async_copy(source, held_ref.at[:, :, pl.ds(n * LANES, LANES)], sems.at[n]))
    pool_as_they_come(copies, sizes, held_ref, pooled_ref)
    pack_side(pooled_ref, slice(0, LANES), 0, left_ref)
    pack_side(pooled_ref, slice(LANES, 2 * LANES), 1, right_ref)


def pool_outer_kernel(
    offsets_ref, merit_ref, near_a_ref, near_b_ref, far_a_ref, far_b_ref, far_west_ref, far_east_ref, more_ref,
    held_ref, pooled_ref, packed_ref, stage_ref, sems, far_sems,
):
    del far_west_ref, far_east_ref
    _, height, width = merit_ref.shape
    blocks = width // LANES
    odd = lax.axis_index("rows") % 2

    def count(v, sign):
        return jnp.maximum(sign * offsets_ref[0, v], 0)

    up, down = 0, 0
    for v in range(VELS):
        up = up + count(v, 1)
        down = down + count(v, -1)

    part = width // 2
    sizes = [(CHUNK, top, part, left) for top in (0, CHUNK) for left in (0, part)]
    copies = []
    for n, (_, top, _, left) in enumerate(sizes):
        rows, cols = pl.ds(top and height - CHUNK, CHUNK), pl.ds(left, part)
        target = held_ref.at[:, pl.ds(top, CHUNK), cols]
        copies.append(pltpu.make_async_copy(merit_ref.at[:, rows, cols], target, sems.at[n]))

    def pack(top, left):
        edge = top // CHUNK
        mine = range(left // LANES, (left + part) // LANES)

        def tile(v, k):
            return pooled_ref[v, edge * CHUNK : (edge + 1) * CHUNK, k * LANES : (k + 1) * LANES].astype(f32)

        if edge == 0:
            at = 0
            for v in range(VELS):
                for k in mine:
                    packed_ref[0, k, pl.ds(at + MAXV, MAXV), :] = tile(v, k)[:MAXV]
                at = at + count(v, -1)
        else:
            at = up
            for v in range(VELS - 1, -1, -1):
                for k in mine:
                    packed_ref[1, k, pl.ds(at, MAXV), :] = tile(v, k)[CHUNK - MAXV :]
                at = at - count(v, 1)

    pool_as_they_come(copies, sizes, held_ref, pooled_ref, pack)

    for slot, ref in enumerate((near_a_ref, near_b_ref)):
        mine = odd if slot == 1 else 1 - odd
        for k in range(blocks):
            piece = packed_ref[mine, k, MAXV : MAXV + SOME_ROWS, :]
            ref[:, k * LANES : (k + 1) * LANES] = piece.astype(bf16)

    more = jnp.maximum(up, down) > SOME_ROWS
    more_ref[0] = more.astype(jnp.int32)

    @pl.when(more)
    def _():
        for slot, ref in enumerate((far_a_ref, far_b_ref)):
            mine = odd if slot == 1 else 1 - odd
            for k in range(blocks):
                piece = packed_ref[mine, k, MAXV + SOME_ROWS : MAXV + ALL_ROWS, :]
                stage_ref[:, k * LANES : (k + 1) * LANES] = piece.astype(bf16)
            copy = pltpu.make_async_copy(stage_ref, ref, far_sems.at[slot])
            copy.start()
            copy.wait()


def pool_cost(merit):
    return pl.CostEstimate(flops=2 * merit.size, bytes_accessed=merit.size, transcendentals=0)


def pool_all(merit, after):
    anywhere = pl.BlockSpec(memory_space=pl.ANY)
    return pl.pallas_call(
        pool_all_kernel,
        out_shape=pltpu.VMEM(merit.shape, bf16),
        in_specs=[anywhere] * (1 + len(after)),
        out_specs=pl.BlockSpec(memory_space=pltpu.VMEM),
        scratch_shapes=[pltpu.VMEM(merit.shape, bf16), pltpu.SemaphoreType.DMA((2 * merit.shape[1] // CHUNK,))],
        cost_estimate=pool_cost(merit),
        compiler_params=params(48 * 2**20),
        name="pool_all",
    )(merit, *after)


def pool_sides(merit, after, far):
    planes, height, _ = merit.shape
    side = (planes * MAXV // LANES, height, LANES)
    anywhere = pl.BlockSpec(memory_space=pl.ANY)
    return pl.pallas_call(
        pool_sides_kernel,
        out_shape=[pltpu.VMEM(side, bf16)] * 2,
        in_specs=[anywhere] * 3,
        out_specs=[pl.BlockSpec(memory_space=pltpu.VMEM)] * 2,
        scratch_shapes=[pltpu.VMEM((planes, height, 2 * LANES), bf16)] * 2 + [pltpu.SemaphoreType.DMA((2,))],
        cost_estimate=brief(),
        compiler_params=params(),
        name="pool_sides",
    )(merit, after, far)


def pool_outer(merit, offsets):
    planes, height, width = merit.shape
    part = (planes, 2 * CHUNK, width)
    near, far = (SOME_ROWS, width), (ALL_ROWS - SOME_ROWS, width)
    return pl.pallas_call(
        pool_outer_kernel,
        out_shape=[pltpu.VMEM(near, bf16)] * 2
        + [pltpu.HBM(far, bf16)] * 2
        + [pltpu.HBM((2 * far[0], LANES), bf16)] * 2
        + [jax.ShapeDtypeStruct((1,), jnp.int32)],
        in_specs=[smem(), pl.BlockSpec(memory_space=pl.ANY)],
        out_specs=[pl.BlockSpec(memory_space=pltpu.VMEM)] * 2 + [pl.BlockSpec(memory_space=pl.ANY)] * 4 + [smem()],
        scratch_shapes=[
            pltpu.VMEM(part, bf16),
            pltpu.VMEM(part, bf16),
            pltpu.VMEM((2, width // LANES, ALL_ROWS + 2 * MAXV, LANES), f32),
            pltpu.VMEM(far, bf16),
            pltpu.SemaphoreType.DMA((4,)),
            pltpu.SemaphoreType.DMA((2,)),
        ],
        cost_estimate=pool_cost(merit),
        compiler_params=params(),
        name="pool_outer",
    )(offsets, merit)


def join_kernel(right_ref, left_ref, a_ref, b_ref, after_ref, last_ref, first_ref):
    del after_ref
    groups, height, _ = right_ref.shape
    width = a_ref.shape[1]
    for side, out, edge in ((right_ref, last_ref, width - LANES), (left_ref, first_ref, 0)):
        for g in range(groups):
            out[g * height : (g + 1) * height, :] = side[g]
        for e, ref in enumerate((a_ref, b_ref)):
            start = groups * height + e * SOME_ROWS
            out[start : start + SOME_ROWS, :] = ref[:, edge : edge + LANES]


def join(right, left, a, b, after):
    groups, height, _ = right.shape
    vmem = pl.BlockSpec(memory_space=pltpu.VMEM)
    return pl.pallas_call(
        join_kernel,
        out_shape=[jax.ShapeDtypeStruct((groups * height + 2 * SOME_ROWS, LANES), bf16)] * 2,
        in_specs=[vmem] * 5,
        out_specs=[vmem] * 2,
        cost_estimate=brief(),
        compiler_params=params(16 * 2**20),
        name="join",
    )(right, left, a, b, after)


def weighted_rows(taps_ref, column_ref, k, count):
    half = taps_ref.shape[0] // 2
    total = jnp.zeros((count, LANES), f32)
    for i in range(taps_ref.shape[0]):
        start = MAXV - half + i
        total = total + taps_ref[i] * column_ref[k, start : start + count, :]
    return total


def merge_kernel(
    offsets_ref, taps_ref, pooled_ref, tile_ref, seam_a_ref, seam_b_ref, near_a_ref, near_b_ref,
    west_ref, east_ref, far_a_ref, far_b_ref, far_west_ref, far_east_ref, out_ref,
    halo_ref, side_ref, column_ref, filtered_ref, moved_ref, at_ref, stage_ref, stage_side_ref, sem,
):
    step = pl.program_id(0)
    planes, height, width = out_ref.shape
    blocks = width // LANES
    groups = VELS * MAXV // LANES
    share = LANES // MAXV
    odd = lax.axis_index("rows") % 2
    cuts = [slice(k * LANES, (k + 1) * LANES) for k in range(blocks)]

    @pl.when(step == 0)
    def _():
        up, down = 0, 0
        for v in range(VELS):
            up = up + jnp.maximum(offsets_ref[0, v], 0)
            down = down + jnp.maximum(-offsets_ref[0, v], 0)
        at_ref[0] = 0
        at_ref[1] = 0
        near = slice(MAXV, MAXV + SOME_ROWS)
        start = groups * height
        for e, ref in enumerate((near_a_ref, near_b_ref)):
            for k in range(blocks):
                halo_ref[e, k + 1, near, :] = ref[:, cuts[k]].astype(f32)
            part = slice(start + e * SOME_ROWS, start + (e + 1) * SOME_ROWS)
            halo_ref[e, 0, near, :] = west_ref[part, :].astype(f32)
            halo_ref[e, blocks + 1, near, :] = east_ref[part, :].astype(f32)
        for e, ref in enumerate((west_ref, east_ref)):
            for g in range(groups):
                side_ref[e, g] = ref[g * height : (g + 1) * height, :].astype(f32)
        for k in range(blocks):
            a, b = seam_a_ref[:, cuts[k]], seam_b_ref[:, cuts[k]]
            column_ref[k, :MAXV, :] = jnp.where(odd == 1, a, b)
            column_ref[k, MAXV : MAXV + height, :] = tile_ref[:, cuts[k]]
            column_ref[k, MAXV + height :, :] = jnp.where(odd == 1, b, a)
        for k in range(blocks):
            filtered_ref[k] = weighted_rows(taps_ref, column_ref, k, height)

        @pl.when(jnp.maximum(up, down) > SOME_ROWS)
        def _():
            def bring(source, target):
                copy = pltpu.make_async_copy(source, target, sem)
                copy.start()
                copy.wait()

            far = slice(MAXV + SOME_ROWS, MAXV + ALL_ROWS)
            count = ALL_ROWS - SOME_ROWS
            for e, ref in enumerate((far_a_ref, far_b_ref)):
                bring(ref, stage_ref)
                for k in range(blocks):
                    halo_ref[e, k + 1, far, :] = stage_ref[:, cuts[k]].astype(f32)
            for k, ref in ((0, far_west_ref), (blocks + 1, far_east_ref)):
                bring(ref, stage_side_ref)
                for e in range(2):
                    halo_ref[e, k, far, :] = stage_side_ref[e * count : (e + 1) * count, :].astype(f32)

    def store(p, rows, turn, pieces):
        lane = lax.broadcasted_iota(jnp.int32, pieces[1].shape, 1)
        before = pieces[0]
        for k in range(1, blocks + 2):
            here = pltpu.roll(pieces[k], turn, 1) if k <= blocks else pieces[k]
            moved_ref[p, k - 1, rows, :] = jnp.where(lane < turn, before, here)
            before = here

    moves = []
    up, down = at_ref[0], at_ref[1]
    for p in range(planes):
        v = step * planes + p
        dy, dx = offsets_ref[0, v], offsets_ref[1, v]
        turn = dx & (LANES - 1)
        q = jnp.where(dx >= 0, 0, 1)
        moves.append((dy, q))
        g, w = v // share, v % share
        shift = (dx - (w + 1 - q) * MAXV) & (LANES - 1)
        beyond = pltpu.roll(side_ref[q, g], shift, 1)
        here = [pooled_ref[v, :, cut].astype(f32) for cut in cuts]
        store(p, slice(MAXV, MAXV + height), turn, [beyond] + here + [beyond])
        below = jnp.where(dy >= 0, 0, 1)
        source = pl.ds(jnp.where(dy >= 0, up + dy, down + MAXV), MAXV)
        halo = [halo_ref[below ^ (1 - odd), k, source, :] for k in range(blocks + 2)]
        halo[0] = pltpu.roll(halo[0], turn, 1)
        halo[-1] = pltpu.roll(halo[-1], turn, 1)
        store(p, pl.ds(pl.multiple_of(below * (MAXV + height), MAXV), MAXV), turn, halo)
        up = up + jnp.maximum(dy, 0)
        down = down + jnp.maximum(-dy, 0)
    at_ref[0] = up
    at_ref[1] = down

    for p in range(planes):
        dy, q = moves[p]
        for k in range(blocks):
            shifted = moved_ref[p, k + q, pl.ds(MAXV - dy, height), :]
            out_ref[p, :, cuts[k]] = (filtered_ref[k] + FORGET * shifted).astype(bf16)


def merge(pooled, tile, seams, nears, sides, fars, offsets, taps_col):
    planes, height, width = pooled.shape
    blocks = width // LANES
    groups = planes * MAXV // LANES
    vmem, anywhere = pl.BlockSpec(memory_space=pltpu.VMEM), pl.BlockSpec(memory_space=pl.ANY)
    return pl.pallas_call(
        merge_kernel,
        grid=(planes // SLAB,),
        out_shape=jax.ShapeDtypeStruct((planes, height, width), bf16),
        in_specs=[smem(), smem()] + [vmem] * 8 + [anywhere] * 4,
        out_specs=pl.BlockSpec((SLAB, height, width), lambda i: (i, 0, 0)),
        scratch_shapes=[
            pltpu.VMEM((2, blocks + 2, ALL_ROWS + 2 * MAXV, LANES), f32),
            pltpu.VMEM((2, groups, height, LANES), f32),
            pltpu.VMEM((blocks, height + 2 * MAXV, LANES), f32),
            pltpu.VMEM((blocks, height, LANES), f32),
            pltpu.VMEM((SLAB, blocks + 1, height + 2 * MAXV, LANES), f32),
            pltpu.SMEM((2,), jnp.int32),
            pltpu.VMEM(fars[0].shape, bf16),
            pltpu.VMEM(fars[2].shape, bf16),
            pltpu.SemaphoreType.DMA,
        ],
        compiler_params=params(40 * 2**20),
        name="merge",
    )(offsets, taps_col, pooled, tile, *seams, *nears, *sides, *fars)


def pass_on(value, axis):
    count = lax.axis_size(axis)
    return lax.ppermute(value, axis, [(i, i + 1) for i in range(count - 1)])


def pass_back(value, axis):
    count = lax.axis_size(axis)
    return lax.ppermute(value, axis, [(i + 1, i) for i in range(count - 1)])


def trade(value, axis, first):
    pairs = []
    for i in range(first, lax.axis_size(axis) - 1, 2):
        pairs += [(i, i + 1), (i + 1, i)]
    return lax.ppermute(value, axis, pairs)


def far_exchange(state):
    count, far_a, far_b, _, _ = state
    far_b = trade(far_b, "rows", 1)
    far_a = trade(far_a, "rows", 0)
    width = far_a.shape[1]
    last = jnp.concatenate([far_a[:, width - LANES :], far_b[:, width - LANES :]], axis=0)
    first = jnp.concatenate([far_a[:, :LANES], far_b[:, :LANES]], axis=0)
    return count - 1, far_a, far_b, pass_on(last, "cols"), pass_back(first, "cols")


def on_device(frame, taps_row, taps_col, merit, offsets):
    _, height, width = merit.shape
    turned = offsets.T
    near_a, near_b, *fars, more = pool_outer(merit, turned)
    b = trade(near_b, "rows", 1)
    a = trade(near_a, "rows", 0)
    pieces = filter_rows(frame, taps_row, frame.shape[1] // width, a)
    tile = lax.all_to_all(pieces, "cols", split_axis=0, concat_axis=0, tiled=True).reshape(height, width)
    _, *fars = lax.while_loop(lambda state: state[0] > 0, far_exchange, (more.reshape(()), *fars))
    right, left = pool_sides(merit, pieces, fars[2])
    top, bottom = tile[:MAXV], tile[height - MAXV :]
    odd = lax.axis_index("rows") % 2 == 1
    for_b, for_a = jnp.where(odd, bottom, top), jnp.where(odd, top, bottom)
    seam_b = trade(for_b, "rows", 1)
    seam_a = trade(for_a, "rows", 0)
    last, first = join(right, left, a, b, for_a)
    west, east = pass_on(last, "cols"), pass_back(first, "cols")
    pooled = pool_all(merit, (for_a, for_b, fars[2], fars[3]))
    return merge(pooled, tile, (seam_a, seam_b), (a, b), (west, east), fars, turned, taps_col)


def solution(mesh):
    in_specs = (P(("rows", "cols"), None), P(), P(), P(None, "rows", "cols"), P())
    out_specs = P(None, "rows", "cols")
    return jax.shard_map(on_device, mesh=mesh, in_specs=in_specs, out_specs=out_specs, check_vma=False)
```
